256 devices in a mesh: bulk: 32 (over x, z_lo, core), row: 8 (over y, z_hi).
Axes of the slice: x: 4, y: 4, z: 8 (z_hi: 2, z_lo: 4; z = z_hi * 4 + z_lo), core: 2. Of those that a mesh axis runs over, the one named last changes fastest.
Arguments:
- charge: float32 [512, 256, 512], P('row', 'bulk'), may hold values from -6 to 6
- green_table: float32 [8, 256, 256], replicated, may hold values from -1 to 2
- shells: int32 [512, 512], P('bulk'), may hold values from 0 to 7, as said below
- planes: int32 [4], replicated, may hold values from 0 to 255
Outputs:
- potential: float32 [512, 256, 512], P('row', 'bulk')
- electrodes: float32 [4, 512, 512], P(None, 'row', 'bulk')
The draws below stay inside these ranges and needn't reach their ends.
Inputs may be any that keep to these rules, and one draw needn't show every extreme that they name: shells[kx, ky] depends only on fx * fx + fy * fy, with fx and fy the signed frequencies of kx and ky, and does not fall as it grows.
All inputs are finite; a program needn't handle non-finite values.
Results may differ from the reference program's by a relative error of at most 0.0003.
Values sent between devices are 32-bit elements; how exact they have to be, the bound alone decides.
A program may use at most 128 MiB of HBM per device.

```python
import math
import jax
import jax.numpy as jnp
from jax import lax

NX = 512
NY = 512
NZ = 256
SHELLS = 8
NPL = 4


def draw_charge(key, part):
    key = jax.random.fold_in(key, 11)
    return jnp.clip(jax.random.normal(key, (NX, NZ, NY), jnp.float32), -6.0, 6.0)


def draw_green_table(key, part):
    key = jax.random.fold_in(key, 23)
    key_spread, key_diagonal = jax.random.split(key)
    identity = jnp.eye(NZ, dtype=jnp.float32)[None, :, :]
    diagonal = jax.random.uniform(key_diagonal, (SHELLS, 1, NZ), jnp.float32, 1.0, 2.0)
    spread = jnp.clip(jax.random.normal(key_spread, (SHELLS, NZ, NZ), jnp.float32), -4.0, 4.0) * (0.5 / math.sqrt(NZ))
    return spread * (1.0 - identity) + diagonal * identity


def draw_shells(key, part):
    key = jax.random.fold_in(key, 37)
    freq_x = jnp.arange(NX, dtype=jnp.int32)
    freq_x = jnp.where(freq_x < NX // 2, freq_x, freq_x - NX)
    freq_y = jnp.arange(NY, dtype=jnp.int32)
    freq_y = jnp.where(freq_y < NY // 2, freq_y, freq_y - NY)
    radius = freq_x[:, None] * freq_x[:, None] + freq_y[None, :] * freq_y[None, :]
    largest = NX // 2 * (NX // 2) + NY // 2 * (NY // 2)
    bounds = jnp.sort(jax.random.randint(key, (SHELLS - 1,), 1, largest + 1))
    return jnp.sum((radius[:, :, None] >= bounds[None, None, :]).astype(jnp.int32), axis=2).astype(jnp.int32)


def plant(entries, rng, smallest, top_value):
    shape = entries.shape
    place = [jax.random.randint(jax.random.fold_in(rng, axis), (), 0, shape[axis]) for axis in range(len(shape))]
    entries = entries.at[tuple(place)].set(smallest)
    longest = shape.index(max(shape))
    place[longest] = (place[longest] + 1) % shape[longest]
    return entries.at[tuple(place)].set(top_value)


def setup_inputs(seed: int = 0) -> dict:
    splits = jax.random.split(jax.random.key(seed), 5)
    return {
        "charge": draw_charge(jax.random.fold_in(splits[4], 71), 0),
        "green_table": draw_green_table(jax.random.fold_in(splits[4], 71), 0),
        "shells": draw_shells(jax.random.fold_in(splits[4], 71), 0),
        "planes": plant(jax.random.randint(splits[3], (NPL,), 0, NZ), jax.random.fold_in(splits[3], 1), 0, NZ - 1).astype(jnp.int32),
    }


def reference(charge, green_table, shells, planes):
    spectrum = jnp.fft.fft2(charge, axes=(0, 2))
    spec_real = jnp.real(spectrum).astype(jnp.float32)
    spec_imag = jnp.imag(spectrum).astype(jnp.float32)

    def apply_shell(carry, shell_index):
        matrix = green_table[shell_index]
        inside = (shells == shell_index)[:, None, :]
        real_in = jnp.where(inside, spec_real, 0.0)
        imag_in = jnp.where(inside, spec_imag, 0.0)
        real_out = carry[0] + jnp.einsum("zw,xwy->xzy", matrix, real_in, precision=lax.Precision.HIGHEST)
        imag_out = carry[1] + jnp.einsum("zw,xwy->xzy", matrix, imag_in, precision=lax.Precision.HIGHEST)
        return (real_out, imag_out), None

    empty_field = jnp.zeros_like(spec_real)
    solved, unused = lax.scan(apply_shell, (empty_field, empty_field), jnp.arange(SHELLS, dtype=jnp.int32))
    potential = jnp.real(jnp.fft.ifft2(solved[0] + 1j * solved[1], axes=(0, 2))).astype(jnp.float32)
    electrodes = jnp.transpose(potential[:, planes, :], (1, 0, 2))
    return potential, electrodes
```

```python
import math

import jax
import jax.numpy as jnp
import numpy as np
from jax import lax
from jax.sharding import PartitionSpec as P

mode = lax.Precision.HIGH


def owned_ky(rows, bulks):
    r = np.arange(rows)[:, None]
    b = np.arange(bulks)[None, :]
    return np.where(b < bulks // 2, 16 * b + r, 16 * (bulks - 1 - b) + 8 + r).reshape(-1)


def tables(n, rows, bulks):
    ky = owned_ky(rows, bulks)
    i = np.arange(n)
    turn = 2.0 * np.pi / n
    angle = turn * (ky[:, None] * i[None, :] % n)
    fwd = np.stack([np.cos(angle), -np.sin(angle)])
    inv = 2.0 * fwd
    zero = np.flatnonzero(ky == 0)[0]
    sign = np.where(i % 2 == 0, 1.0, -1.0)
    fwd[0, zero], fwd[1, zero] = 1.0, sign
    inv[0, zero], inv[1, zero] = 1.0, sign
    inv = inv / (n * n)
    angle = turn * (i[:, None] * i[None, :] % n)
    c, s = np.cos(angle), np.sin(angle)
    full = np.array([[c, -s], [s, c]])
    half = np.where(i[None, :] <= n // 2, c, s) * np.sqrt(2.0)
    half[:, 0], half[:, n // 2] = 1.0, sign
    none = np.zeros_like(half)
    packed = np.array([[half, none], [none, half]])
    both = []
    for m in (full, packed):
        m = m.transpose(0, 2, 1, 3).reshape(2, rows, n // rows, 2 * n)
        both.append(m.transpose(1, 0, 2, 3).reshape(2 * n, 2 * n))
    return fwd.astype(np.float32), inv.astype(np.float32), np.stack(both).astype(np.float32)


def local(charge, green, shells, planes):
    nxl, nzl, n = charge.shape
    rows, bulks = lax.axis_size("row"), lax.axis_size("bulk")
    r, b = lax.axis_index("row"), lax.axis_index("bulk")
    fwd, inv, mats = tables(n, rows, bulks)
    devices = rows * bulks
    axes = ("row", "bulk")
    own = jnp.where(b < bulks // 2, r, 8 - r)
    row_own = lax.dynamic_slice_in_dim(shells, own, 1, 0)
    row_far = lax.ppermute(shells[:1], "bulk", [(bulks // 2, 0)])
    first = (r == 0) & (b == 0)
    labels = jnp.concatenate([row_own, jnp.where(first, row_far, row_own)], axis=1)
    mat = lax.dynamic_index_in_dim(jnp.asarray(mats), first.astype(jnp.int32), 0, keepdims=False)

    sent = jnp.einsum("rdy,xzy->dzrx", fwd, charge, precision=mode).reshape(devices, nzl, 2 * nxl)
    got = lax.all_to_all(sent, axes, 0, 0, tiled=True)
    cols = got.reshape(rows, bulks * nzl, 2 * nxl).transpose(1, 0, 2).reshape(bulks * nzl, 2 * n)
    spec = jnp.dot(cols, mat, precision=mode)
    solved = jnp.zeros_like(spec)
    for s in range(green.shape[0]):
        solved = solved + jnp.dot(green[s], jnp.where(labels == s, spec, 0.0), precision=mode)
    back = lax.dot_general(solved, mat, (((1,), (1,)), ((), ())), precision=mode)
    picked = jnp.take(back, planes, axis=0).reshape(4, rows, 2, 8, 8)
    picked = picked.transpose(1, 0, 3, 2, 4).reshape(devices, 2, 8)
    back = back.reshape(bulks * nzl, rows, 2 * nxl).transpose(1, 0, 2).reshape(devices, nzl, 2 * nxl)
    home = lax.all_to_all(back, axes, 0, 0, tiled=True).reshape(devices, nzl, 2, nxl)
    field = jnp.einsum("dzrx,rdy->xzy", home, inv, precision=mode)
    part = lax.all_to_all(picked, axes, 0, 0, tiled=True)
    part = jnp.einsum("drx,rdy->xy", part, inv, precision=mode)
    part = part.reshape(8, bulks, n // bulks).transpose(1, 0, 2)
    part = lax.all_to_all(part, "bulk", 0, 0, tiled=True)
    return field, part.reshape(4, 8 * 8, n // bulks)


def solution(mesh):
    placed = (P("row", "bulk", None), P(), P("bulk", None), P())
    return jax.shard_map(
        local,
        mesh=mesh,
        in_specs=placed,
        out_specs=(P("row", "bulk", None), P(None, "row", "bulk")),
        check_vma=False,
    )
```

```python
import functools

import jax
import jax.numpy as jnp
import ml_dtypes
import numpy as np
from jax import lax
from jax.experimental import pallas as pl
from jax.experimental.pallas import tpu as pltpu
from jax.sharding import PartitionSpec as P

MESH = pl.DeviceIdType.MESH
ROWS, BULKS = 8, 32
DEVICES = ROWS * BULKS
HALF = DEVICES // 2
N = 512
NZ = 256
HOT = 10


def owned_ky():
    r = np.arange(ROWS)[:, None]
    b = np.arange(BULKS)[None, :]
    return np.where(b < BULKS // 2, 16 * b + r, 16 * (BULKS - 1 - b) + 8 + r).reshape(-1)


def split_table(a):
    a = np.asarray(a, np.float64)
    hi = a.astype(np.float32).astype(ml_dtypes.bfloat16)
    lo = (a - hi.astype(np.float64)).astype(np.float32).astype(ml_dtypes.bfloat16)
    return np.stack([hi, lo])


def tables():
    n = N
    ky = owned_ky()
    i = np.arange(n)
    turn = 2.0 * np.pi / n
    angle = turn * (ky[:, None] * i[None, :] % n)
    fwd = np.stack([np.cos(angle), -np.sin(angle)])
    inv = 2.0 * fwd
    zero = np.flatnonzero(ky == 0)[0]
    sign = np.where(i % 2 == 0, 1.0, -1.0)
    fwd[0, zero], fwd[1, zero] = 1.0, sign
    inv[0, zero], inv[1, zero] = 1.0, sign
    inv = inv / (n * n)
    angle = turn * (i[:, None] * i[None, :] % n)
    c, s = np.cos(angle), np.sin(angle)
    full = np.array([[c, -s], [s, c]])
    half = np.where(i[None, :] <= n // 2, c, s) * np.sqrt(2.0)
    half[:, 0], half[:, n // 2] = 1.0, sign
    none = np.zeros_like(half)
    packed = np.array([[half, none], [none, half]])
    both = []
    for m in (full, packed):
        m = m.transpose(0, 2, 1, 3).reshape(2, ROWS, n // ROWS, 2 * n)
        both.append(m.transpose(1, 0, 2, 3).reshape(2 * n, 2 * n))
    both = np.stack(both)
    mats = split_table(both).transpose(1, 0, 2, 3)
    mats_t = split_table(both.transpose(0, 2, 1)).transpose(1, 0, 2, 3)
    fwd = split_table(fwd.reshape(2 * DEVICES, n))
    inv_t = split_table(inv.transpose(0, 2, 1).reshape(2 * n, DEVICES))
    inv = split_table(inv.reshape(2 * DEVICES, n))
    return fwd, mats, mats_t, inv, inv_t


def parts(x):
    hi = x.astype(jnp.bfloat16)
    lo = (x - hi.astype(jnp.float32)).astype(jnp.bfloat16)
    return hi, lo


def dot(a, b, dims=((1,), (0,))):
    return lax.dot_general(a, b, (dims, ((), ())), preferred_element_type=jnp.float32)


def dot3(ah, al, bh, bl, dims=((1,), (0,))):
    return dot(ah, bh, dims) + dot(ah, bl, dims) + dot(al, bh, dims)


def kernel(
    charge, fwd, shells, planes, green, mats, mats_t, inv, inv_t,
    out, electrodes,
    sbuf, rbuf, obuf, home, mat, mat_t, inv_v, inv_t_v, g32, g_hi, g_lo, x_hi, x_lo, v_hi, v_lo,
    lab, lab_src, lab_far, ebuf, erecv, eout, elrecv,
    table_sem, ssem, rsem, hssem, hrsem, essem, ersem, elssem, elrsem, lssem, lrsem,
):
    r, b = lax.axis_index("row"), lax.axis_index("bulk")
    m = r * BULKS + b
    core = lax.rem(b, 2)
    first = m == 0
    feeder = m == BULKS // 2
    hot = lax.rem(b, HOT) == 0

    def at(d):
        return {"row": lax.div(d, BULKS), "bulk": lax.rem(d, BULKS)}

    def tile(ref, d):
        return ref.at[pl.ds(pl.multiple_of(d * 8, 8), 8), :]

    def push(src, dst, d, ss, rs):
        return pltpu.make_async_remote_copy(
            src_ref=src, dst_ref=dst, send_sem=ss, recv_sem=rs, device_id=at(d), device_id_type=MESH
        )

    def drain(ref, sem):
        pltpu.make_async_copy(ref, ref, sem).wait()

    barrier = pltpu.get_barrier_semaphore()

    def greet(i, c):
        pl.semaphore_signal(barrier, inc=1, device_id=at(lax.rem(m + i, DEVICES)), device_id_type=MESH)
        return c

    lax.fori_loop(1, DEVICES, greet, 0)

    which = jnp.where(first, 1, 0)
    loads = [
        pltpu.make_async_copy(src, dst, table_sem.at[i])
        for i, (src, dst) in enumerate(
            [(green, g32), (mats.at[which], mat), (mats_t.at[which], mat_t), (inv, inv_v), (inv_t, inv_t_v)]
        )
    ]
    for load in loads:
        load.start()

    lane = lax.broadcasted_iota(jnp.int32, (DEVICES, 128), 1)
    for q in range(2):
        rows = jnp.concatenate([charge[:, 4 * q + j, :] for j in range(4)], axis=0)
        c_hi, c_lo = parts(rows)
        spec = dot3(fwd[0], fwd[1], c_hi, c_lo, ((1,), (1,)))
        for p in range(2):
            re = spec[:DEVICES, 128 * p : 128 * (p + 1)]
            im = spec[DEVICES:, 128 * p : 128 * (p + 1)]
            z = 4 * q + 2 * p
            sbuf[pl.ds(z, DEVICES, stride=8), :] = jnp.where(lane < 64, re, pltpu.roll(im, 64, 1))
            sbuf[pl.ds(z + 1, DEVICES, stride=8), :] = jnp.where(lane < 64, pltpu.roll(re, 64, 1), im)

    own = shells[pl.ds(jnp.where(b < BULKS // 2, r, 8 - r), 1), :]
    lab[:, :N] = own
    lab_src[...] = shells[0:1, :]

    pl.semaphore_wait(barrier, DEVICES - 1)

    keep = pltpu.make_async_copy(tile(sbuf, m), tile(rbuf, m), rsem)
    keep.start()
    pair = lax.div(m, 2)
    for c in range(2):

        @pl.when(core != c)
        def _(c=c):
            d = 2 * pair + c
            push(tile(sbuf, d), tile(rbuf, m), d, ssem, rsem).start()

        def send(j, carry, c=c):
            d = 2 * lax.rem(pair + j, HALF) + c
            push(tile(sbuf, d), tile(rbuf, m), d, ssem, rsem).start()
            return carry

        lax.fori_loop(1, HALF, send, 0)

    @pl.when(feeder)
    def _():
        push(lab_src, lab_far, 0, lssem, lrsem).start()

    loads[0].wait()
    for s in range(8):
        hi, lo = parts(g32[s])
        g_hi[s] = hi
        g_lo[s] = lo
    loads[1].wait()
    loads[2].wait()

    @pl.when(feeder)
    def _():
        drain(lab_src, lssem)

    @pl.when(first)
    def _():
        drain(lab_far, lrsem)
        lab[:, N:] = lab_far[...]

    @pl.when(jnp.logical_not(first))
    def _():
        lab[:, N:] = lab[:, :N]

    drain(rbuf, rsem)

    for k in range(ROWS):
        hi, lo = parts(rbuf[pl.ds(k * NZ, NZ), :])
        x_hi[:, k * 128 : (k + 1) * 128] = hi
        x_lo[:, k * 128 : (k + 1) * 128] = lo

    def solve(t, carry):
        cols = pl.ds(pl.multiple_of(t * 256, 256), 256)
        spec = dot3(x_hi[...], x_lo[...], mat[0, :, cols], mat[1, :, cols])
        s_hi, s_lo = parts(spec)
        label = lab[:, cols]

        acc = jnp.zeros((NZ, 256), jnp.float32)
        for s in range(8):
            mask = label == s
            m_hi = jnp.where(mask, s_hi, jnp.zeros_like(s_hi))
            m_lo = jnp.where(mask, s_lo, jnp.zeros_like(s_lo))
            acc = acc + dot3(g_hi[s], g_lo[s], m_hi, m_lo)
        hi, lo = parts(acc)
        v_hi[:, cols] = hi
        v_lo[:, cols] = lo
        return carry

    lax.fori_loop(0, 4, solve, 0)

    hkeep = pltpu.make_async_copy(tile(obuf, m), tile(home, m), hrsem)
    y = lax.div(r, 2)

    def give(t, carry):
        g = lax.rem(y + t, 4)
        cols = pl.ds(pl.multiple_of(g * 256, 256), 256)
        back = dot3(v_hi[...], v_lo[...], mat_t[0, :, cols], mat_t[1, :, cols])
        for h in range(2):
            obuf[pl.ds(pl.multiple_of((2 * g + h) * NZ, NZ), NZ), :] = back[:, h * 128 : (h + 1) * 128]
        for h in range(2):
            for p in range(4):
                k = (2 * g + h) * 4 + p
                ebuf[k] = obuf[pl.ds((2 * g + h) * NZ + planes[p], 1), :]
                d = (2 * g + h) * BULKS + HOT * p

                @pl.when(d != m)
                def _():
                    push(ebuf.at[k], erecv.at[m], d, essem, ersem).start()

                @pl.when(d == m)
                def _():
                    pltpu.make_async_copy(ebuf.at[k], erecv.at[m], ersem).start()

        @pl.when(t == 0)
        def _():
            hkeep.start()

        base = lax.rem(m, 64)

        def send(j, c):
            d = g * 64 + lax.rem(base + j, 64)
            push(tile(obuf, d), tile(home, m), d, hssem, hrsem).start()
            return c

        lax.fori_loop(jnp.where(t == 0, 1, 0), 64, send, 0)
        return carry

    lax.fori_loop(0, 4, give, 0)
    loads[3].wait()
    loads[4].wait()

    @pl.when(hot)
    def _():
        drain(erecv, ersem)
        e_hi, e_lo = parts(erecv[...].reshape(DEVICES, 128))
        both = dot3(inv_t_v[0], inv_t_v[1], e_hi, e_lo)
        eout[...] = both[:N] + pltpu.roll(both[N:], 64, 1)
        p = lax.div(b, HOT)

        def spread(j, c):
            d = r * BULKS + lax.rem(b + j, BULKS)
            src = eout.at[pl.ds(pl.multiple_of(lax.rem(d, BULKS) * 16, 16), 16), :]
            push(src, elrecv.at[p], d, elssem, elrsem).start()
            return c

        pltpu.make_async_copy(eout.at[pl.ds(pl.multiple_of(b * 16, 16), 16), :], elrecv.at[p], elrsem).start()
        lax.fori_loop(1, BULKS, spread, 0)

    drain(home, hrsem)
    for q in range(2):
        re, im = [], []
        for j in range(4):
            flip = jnp.transpose(home[pl.ds(4 * q + j, DEVICES, stride=8), :])
            re.append(flip[:64])
            im.append(flip[64:])
        w_hi, w_lo = parts(jnp.concatenate([jnp.concatenate(re, axis=0), jnp.concatenate(im, axis=0)], axis=1))
        field = dot3(w_hi, w_lo, inv_v[0], inv_v[1])
        for j in range(4):
            out[:, 4 * q + j, :] = field[64 * j : 64 * (j + 1)]

    drain(elrecv, elrsem)
    for p in range(4):
        electrodes[p] = jnp.transpose(elrecv[p])[:64, :]

    drain(sbuf.at[pl.ds(0, 8 * (DEVICES - 1)), :], ssem)
    drain(obuf.at[pl.ds(0, 8 * (DEVICES - 1)), :], hssem)
    drain(ebuf.at[pl.ds(0, 31)], essem)

    @pl.when(jnp.logical_not(hot))
    def _():
        drain(ebuf.at[0], essem)

    @pl.when(hot)
    def _():
        drain(eout.at[pl.ds(0, 16 * (BULKS - 1)), :], elssem)


def local(charge, green, shells, planes):
    fwd, mats, mats_t, inv, inv_t = (jnp.asarray(t) for t in tables())
    f32, bf16 = jnp.float32, jnp.bfloat16
    vmem, hbm = pl.BlockSpec(memory_space=pltpu.VMEM), pl.BlockSpec(memory_space=pl.ANY)
    dma = pltpu.SemaphoreType.DMA
    return pl.pallas_call(
        kernel,
        out_shape=(
            jax.ShapeDtypeStruct(charge.shape, f32),
            jax.ShapeDtypeStruct((4, N // ROWS, N // BULKS), f32),
        ),
        in_specs=[vmem, vmem, vmem, pl.BlockSpec(memory_space=pltpu.SMEM), hbm, hbm, hbm, hbm, hbm],
        out_specs=(vmem, vmem),
        scratch_shapes=[
            pltpu.VMEM((8 * DEVICES, 128), f32),
            pltpu.VMEM((8 * DEVICES, 128), f32),
            pltpu.VMEM((8 * DEVICES, 128), f32),
            pltpu.VMEM((8 * DEVICES, 128), f32),
            pltpu.VMEM((2, 2 * N, 2 * N), bf16),
            pltpu.VMEM((2, 2 * N, 2 * N), bf16),
            pltpu.VMEM((2, 2 * DEVICES, N), bf16),
            pltpu.VMEM((2, 2 * N, DEVICES), bf16),
            pltpu.VMEM((8, NZ, NZ), f32),
            pltpu.VMEM((8, NZ, NZ), bf16),
            pltpu.VMEM((8, NZ, NZ), bf16),
            pltpu.VMEM((NZ, 2 * N), bf16),
            pltpu.VMEM((NZ, 2 * N), bf16),
            pltpu.VMEM((NZ, 2 * N), bf16),
            pltpu.VMEM((NZ, 2 * N), bf16),
            pltpu.VMEM((1, 2 * N), jnp.int32),
            pltpu.VMEM((1, N), jnp.int32),
            pltpu.VMEM((1, N), jnp.int32),
            pltpu.VMEM((32, 1, 128), f32),
            pltpu.VMEM((DEVICES, 1, 128), f32),
            pltpu.VMEM((N, 128), f32),
            pltpu.VMEM((4, 16, 128), f32),
            dma((5,)),
        ]
        + [dma] * 10,
        compiler_params=pltpu.CompilerParams(
            collective_id=0, has_side_effects=True, vmem_limit_bytes=48 * 1024 * 1024
        ),
    )(charge, fwd, shells, planes, green, mats, mats_t, inv, inv_t)


def solution(mesh):
    placed = (P("row", "bulk", None), P(), P("bulk", None), P())
    return jax.shard_map(
        local,
        mesh=mesh,
        in_specs=placed,
        out_specs=(P("row", "bulk", None), P(None, "row", "bulk")),
        check_vma=False,
    )
```

```python
import functools

import jax
import jax.numpy as jnp
import ml_dtypes
import numpy as np
from jax import lax
from jax.experimental import pallas as pl
from jax.experimental.pallas import tpu as pltpu
from jax.sharding import PartitionSpec as P

MESH = pl.DeviceIdType.MESH
ROWS, BULKS = 8, 32
DEVICES = ROWS * BULKS
HALF = DEVICES // 2
N = 512
NZ = 256
HOT = 10


def owned_ky():
    r = np.arange(ROWS)[:, None]
    b = np.arange(BULKS)[None, :]
    return np.where(b < BULKS // 2, 16 * b + r, 16 * (BULKS - 1 - b) + 8 + r).reshape(-1)


def split_table(a):
    a = np.asarray(a, np.float64)
    hi = a.astype(np.float32).astype(ml_dtypes.bfloat16)
    lo = (a - hi.astype(np.float64)).astype(np.float32).astype(ml_dtypes.bfloat16)
    return np.stack([hi, lo])


def tables():
    n = N
    ky = owned_ky()
    i = np.arange(n)
    turn = 2.0 * np.pi / n
    angle = turn * (ky[:, None] * i[None, :] % n)
    fwd = np.stack([np.cos(angle), -np.sin(angle)])
    inv = 2.0 * fwd
    zero = np.flatnonzero(ky == 0)[0]
    sign = np.where(i % 2 == 0, 1.0, -1.0)
    fwd[0, zero], fwd[1, zero] = 1.0, sign
    inv[0, zero], inv[1, zero] = 1.0, sign
    inv = inv / (n * n)
    angle = turn * (i[:, None] * i[None, :] % n)
    c, s = np.cos(angle), np.sin(angle)
    full = np.array([[c, -s], [s, c]])
    half = np.where(i[None, :] <= n // 2, c, s) * np.sqrt(2.0)
    half[:, 0], half[:, n // 2] = 1.0, sign
    none = np.zeros_like(half)
    packed = np.array([[half, none], [none, half]])
    both = []
    for m in (full, packed):
        m = m.transpose(0, 2, 1, 3).reshape(2, ROWS, n // ROWS, 2 * n)
        both.append(m.transpose(1, 0, 2, 3).reshape(2 * n, 2 * n))
    both = np.stack(both)
    mats = split_table(both).transpose(1, 0, 2, 3)
    mats_t = split_table(both.transpose(0, 2, 1)).transpose(1, 0, 2, 3)
    fwd = split_table(fwd.reshape(2 * DEVICES, n))
    inv_t = split_table(inv.transpose(0, 2, 1).reshape(2 * n, DEVICES))
    inv = split_table(inv.reshape(2, HALF, 2, n).transpose(2, 0, 1, 3).reshape(2, DEVICES, n))
    return fwd, mats, mats_t, inv, inv_t


def parts(x):
    hi = x.astype(jnp.bfloat16)
    lo = (x - hi.astype(jnp.float32)).astype(jnp.bfloat16)
    return hi, lo


def dot(a, b, dims=((1,), (0,))):
    return lax.dot_general(a, b, (dims, ((), ())), preferred_element_type=jnp.float32)


def dot3(ah, al, bh, bl, dims=((1,), (0,))):
    return dot(ah, bh, dims) + dot(ah, bl, dims) + dot(al, bh, dims)


def kernel(
    charge_h, fwd_h, shells_h, planes_h, green, mats, mats_t, inv, inv_t,
    out, electrodes,
    charge, fwd, shells, planes,
    sbuf, rbuf, obuf, home, mat, mat_t, inv_v, inv_t_v, g32, g_hi, g_lo, spec_ref, v_hi, v_lo, field_ref,
    lab, lab_src, lab_far, ebuf, erecv, eout, elrecv,
    gate, table_sem, ssem, rsem, hssem, hrsem, essem, ersem, elssem, elrsem, lssem, lrsem,
):
    r, b = lax.axis_index("row"), lax.axis_index("bulk")
    m = r * BULKS + b
    core = lax.rem(b, 2)
    pair = lax.div(m, 2)
    y, q0 = lax.div(pair, 32), lax.rem(pair, 32)
    first = m == 0
    feeder = m == BULKS // 2
    hot = lax.rem(b, HOT) == 0

    def at(d):
        return {"row": lax.div(d, BULKS), "bulk": lax.rem(d, BULKS)}

    def tile(ref, d):
        return ref.at[pl.ds(pl.multiple_of(d * 8, 8), 8), :]

    def push(src, dst, d, ss, rs):
        return pltpu.make_async_remote_copy(
            src_ref=src, dst_ref=dst, send_sem=ss, recv_sem=rs, device_id=at(d), device_id_type=MESH
        )

    def drain(ref, sem):
        pltpu.make_async_copy(ref, ref, sem).wait()

    which = jnp.where(first, 1, 0)
    moves = [
        (charge_h, charge), (fwd_h, fwd), (shells_h, shells), (planes_h, planes), (green, g32),
        (mats.at[which], mat), (mats_t.at[which], mat_t), (inv, inv_v), (inv_t, inv_t_v),
    ]
    loads = [pltpu.make_async_copy(src, dst, table_sem.at[i]) for i, (src, dst) in enumerate(moves)]
    for load in loads[:4]:
        load.start()

    barrier = pltpu.get_barrier_semaphore()
    z = lax.rem(r, 2) * 4 + lax.rem(lax.div(b, 2), 4)
    x = lax.div(b, 8)

    def place(px, py, pz, pc):
        return {"row": py * 2 + lax.div(pz, 4), "bulk": px * 8 + lax.rem(pz, 4) * 2 + pc}

    plane_peers = [place(lax.rem(x + i, 4), lax.rem(y + j, 4), z, core) for i in range(4) for j in range(4) if i + j]
    line_peers = [place(x, y, lax.rem(z + i, 8), lax.rem(core + j, 2)) for i in range(8) for j in range(2) if i + j]
    for peer in plane_peers + line_peers:
        pl.semaphore_signal(barrier, inc=1, device_id=peer, device_id_type=MESH)
    for load in loads[4:]:
        load.start()

    loads[0].wait()
    loads[1].wait()
    lane = lax.broadcasted_iota(jnp.int32, (DEVICES, 128), 1)
    for q in range(2):
        rows = jnp.concatenate([charge[:, 4 * q + j, :] for j in range(4)], axis=0)
        c_hi, c_lo = parts(rows)
        spec = dot3(fwd[0], fwd[1], c_hi, c_lo, ((1,), (1,)))
        for p in range(2):
            re = spec[:DEVICES, 128 * p : 128 * (p + 1)]
            im = spec[DEVICES:, 128 * p : 128 * (p + 1)]
            k = 4 * q + 2 * p
            sbuf[pl.ds(k, DEVICES, stride=8), :] = jnp.where(lane < 64, re, pltpu.roll(im, 64, 1))
            sbuf[pl.ds(k + 1, DEVICES, stride=8), :] = jnp.where(lane < 64, pltpu.roll(re, 64, 1), im)

    loads[2].wait()
    loads[3].wait()
    lab[:, :N] = shells[pl.ds(jnp.where(b < BULKS // 2, r, 8 - r), 1), :]
    lab_src[...] = shells[0:1, :]

    pl.semaphore_wait(barrier, len(plane_peers) + len(line_peers))
    for peer in line_peers:
        pl.semaphore_signal(gate, inc=1, device_id=peer, device_id_type=MESH)
    pl.semaphore_wait(gate, len(line_peers))

    pltpu.make_async_copy(tile(sbuf, m), tile(rbuf, m), rsem.at[y]).start()
    for c in range(2):

        @pl.when(core != c)
        def _(c=c):
            d = 2 * pair + c
            push(tile(sbuf, d), tile(rbuf, m), d, ssem, rsem.at[y]).start()

        def send(i, carry, c=c):
            t, j = lax.div(i, 32), lax.rem(i, 32)
            d = 2 * (lax.rem(y + t, 4) * 32 + lax.rem(q0 + j, 32)) + c
            push(tile(sbuf, d), tile(rbuf, m), d, ssem, rsem.at[y]).start()
            return carry

        lax.fori_loop(1, HALF, send, 0)

    @pl.when(feeder)
    def _():
        push(lab_src, lab_far, 0, lssem, lrsem).start()

    loads[4].wait()
    for s in range(8):
        hi, lo = parts(g32[s])
        g_hi[s] = hi
        g_lo[s] = lo
    loads[5].wait()
    loads[6].wait()

    @pl.when(feeder)
    def _():
        drain(lab_src, lssem)

    @pl.when(first)
    def _():
        drain(lab_far, lrsem)
        lab[:, N:] = lab_far[...]

    @pl.when(jnp.logical_not(first))
    def _():
        lab[:, N:] = lab[:, :N]

    spec_ref[...] = jnp.zeros_like(spec_ref)

    def gather(t, carry):
        g = lax.rem(y + 4 - t, 4)
        drain(rbuf.at[pl.ds(pl.multiple_of(g * 512, 512), 512), :], rsem.at[g])
        rows = [rbuf[pl.ds(pl.multiple_of(g * 512 + h * NZ, NZ), NZ), :] for h in range(2)]
        hi, lo = parts(jnp.concatenate(rows, axis=1))
        deep = pl.ds(pl.multiple_of(g * 256, 256), 256)
        spec_ref[...] += dot3(hi, lo, mat[0, deep, :], mat[1, deep, :])
        return carry

    lax.fori_loop(0, 4, gather, 0)

    def solve(t, carry):
        cols = pl.ds(pl.multiple_of(t * 256, 256), 256)
        s_hi, s_lo = parts(spec_ref[:, cols])
        label = lab[:, cols]
        acc = jnp.zeros((NZ, 256), jnp.float32)
        for s in range(8):
            mask = label == s
            m_hi = jnp.where(mask, s_hi, jnp.zeros_like(s_hi))
            m_lo = jnp.where(mask, s_lo, jnp.zeros_like(s_lo))
            acc = acc + dot3(g_hi[s], g_lo[s], m_hi, m_lo)
        hi, lo = parts(acc)
        v_hi[:, cols] = hi
        v_lo[:, cols] = lo
        return carry

    lax.fori_loop(0, 4, solve, 0)

    spot = core * HALF + pair

    def give(t, carry):
        g = lax.rem(y + t, 4)
        cols = pl.ds(pl.multiple_of(g * 256, 256), 256)
        back = dot3(v_hi[...], v_lo[...], mat_t[0, :, cols], mat_t[1, :, cols])
        for h in range(2):
            obuf[pl.ds(pl.multiple_of((2 * g + h) * NZ, NZ), NZ), :] = back[:, h * 128 : (h + 1) * 128]
        for h in range(2):
            for p in range(4):
                k = (2 * g + h) * 4 + p
                ebuf[k] = obuf[pl.ds((2 * g + h) * NZ + planes[p], 1), :]
                d = (2 * g + h) * BULKS + HOT * p

                @pl.when(d != m)
                def _():
                    push(ebuf.at[k], erecv.at[m], d, essem, ersem).start()

                @pl.when(d == m)
                def _():
                    pltpu.make_async_copy(ebuf.at[k], erecv.at[m], ersem).start()

        @pl.when(t == 0)
        def _():
            pltpu.make_async_copy(tile(obuf, m), tile(home, spot), hrsem.at[core]).start()
            d = m + 1 - 2 * core
            push(tile(obuf, d), tile(home, spot), d, hssem, hrsem.at[core]).start()

        def send(j, c):
            d = 2 * (g * 32 + lax.rem(q0 + j, 32))
            push(tile(obuf, d), tile(home, spot), d, hssem, hrsem.at[core]).start()
            push(tile(obuf, d + 1), tile(home, spot), d + 1, hssem, hrsem.at[core]).start()
            return c

        lax.fori_loop(jnp.where(t == 0, 1, 0), 32, send, 0)
        return carry

    lax.fori_loop(0, 4, give, 0)
    loads[7].wait()
    loads[8].wait()

    def regain(c):
        drain(home.at[pl.ds(c * 8 * HALF, 8 * HALF), :], hrsem.at[c])
        re, im = [], []
        for k in range(8):
            flip = jnp.transpose(home[pl.ds(c * 8 * HALF + k, HALF, stride=8), :])
            re.append(flip[:64])
            im.append(flip[64:])
        w_hi, w_lo = parts(jnp.concatenate([jnp.concatenate(re, axis=0), jnp.concatenate(im, axis=0)], axis=1))
        return dot3(w_hi, w_lo, inv_v[0, c], inv_v[1, c])

    field_ref[...] = regain(0)

    @pl.when(hot)
    def _():
        drain(erecv, ersem)
        e_hi, e_lo = parts(erecv[...].reshape(DEVICES, 128))
        both = dot3(inv_t_v[0], inv_t_v[1], e_hi, e_lo)
        eout[...] = both[:N] + pltpu.roll(both[N:], 64, 1)
        p = lax.div(b, HOT)

        def spread(j, c):
            d = r * BULKS + lax.rem(b + j, BULKS)
            src = eout.at[pl.ds(pl.multiple_of(lax.rem(d, BULKS) * 16, 16), 16), :]
            push(src, elrecv.at[p], d, elssem, elrsem).start()
            return c

        pltpu.make_async_copy(eout.at[pl.ds(pl.multiple_of(b * 16, 16), 16), :], elrecv.at[p], elrsem).start()
        lax.fori_loop(1, BULKS, spread, 0)

    rest = regain(1)
    for k in range(8):
        out[:, k, :] = field_ref[64 * k : 64 * (k + 1), :] + rest[64 * k : 64 * (k + 1)]

    drain(elrecv, elrsem)
    electrodes[...] = elrecv[:, :, :64]

    drain(sbuf.at[pl.ds(0, 8 * (DEVICES - 1)), :], ssem)
    drain(obuf.at[pl.ds(0, 8 * (DEVICES - 1)), :], hssem)
    drain(ebuf.at[pl.ds(0, 31)], essem)

    @pl.when(jnp.logical_not(hot))
    def _():
        drain(ebuf.at[0], essem)

    @pl.when(hot)
    def _():
        drain(eout.at[pl.ds(0, 16 * (BULKS - 1)), :], elssem)


def local(charge, green, shells, planes):
    fwd, mats, mats_t, inv, inv_t = (jnp.asarray(t) for t in tables())
    f32, bf16, i32 = jnp.float32, jnp.bfloat16, jnp.int32
    vmem, hbm = pl.BlockSpec(memory_space=pltpu.VMEM), pl.BlockSpec(memory_space=pltpu.HBM)
    dma = pltpu.SemaphoreType.DMA
    field, plates = pl.pallas_call(
        kernel,
        out_shape=(
            jax.ShapeDtypeStruct(charge.shape, f32),
            jax.ShapeDtypeStruct((4, N // BULKS, N // ROWS), f32),
        ),
        in_specs=[hbm] * 9,
        out_specs=(vmem, vmem),
        scratch_shapes=[
            pltpu.VMEM(charge.shape, f32),
            pltpu.VMEM(fwd.shape, bf16),
            pltpu.VMEM(shells.shape, i32),
            pltpu.SMEM(planes.shape, i32),
            pltpu.VMEM((8 * DEVICES, 128), f32),
            pltpu.VMEM((8 * DEVICES, 128), f32),
            pltpu.VMEM((8 * DEVICES, 128), f32),
            pltpu.VMEM((8 * DEVICES, 128), f32),
            pltpu.VMEM(mats.shape[1:], bf16),
            pltpu.VMEM(mats.shape[1:], bf16),
            pltpu.VMEM(inv.shape, bf16),
            pltpu.VMEM(inv_t.shape, bf16),
            pltpu.VMEM((8, NZ, NZ), f32),
            pltpu.VMEM((8, NZ, NZ), bf16),
            pltpu.VMEM((8, NZ, NZ), bf16),
            pltpu.VMEM((NZ, 2 * N), f32),
            pltpu.VMEM((NZ, 2 * N), bf16),
            pltpu.VMEM((NZ, 2 * N), bf16),
            pltpu.VMEM((N, N), f32),
            pltpu.VMEM((1, 2 * N), i32),
            pltpu.VMEM((1, N), i32),
            pltpu.VMEM((1, N), i32),
            pltpu.VMEM((32, 1, 128), f32),
            pltpu.VMEM((DEVICES, 1, 128), f32),
            pltpu.VMEM((N, 128), f32),
            pltpu.VMEM((4, 16, 128), f32),
            pltpu.SemaphoreType.REGULAR,
            dma((9,)),
            dma,
            dma((4,)),
            dma,
            dma((2,)),
        ]
        + [dma] * 6,
        compiler_params=pltpu.CompilerParams(
            collective_id=0, has_side_effects=True, vmem_limit_bytes=48 * 1024 * 1024
        ),
    )(charge, fwd, shells, planes, green, mats, mats_t, inv, inv_t)
    return field, jnp.transpose(plates, (0, 2, 1))


def solution(mesh):
    placed = (P("row", "bulk", None), P(), P("bulk", None), P())
    return jax.shard_map(
        local,
        mesh=mesh,
        in_specs=placed,
        out_specs=(P("row", "bulk", None), P(None, "row", "bulk")),
        check_vma=False,
    )
```

```python
import functools

import jax
import jax.numpy as jnp
import ml_dtypes
import numpy as np
from jax import lax
from jax.experimental import pallas as pl
from jax.experimental.pallas import tpu as pltpu
from jax.sharding import PartitionSpec as P

MESH = pl.DeviceIdType.MESH
ROWS, BULKS = 8, 32
DEVICES = ROWS * BULKS
HALF = DEVICES // 2
N = 512
NZ = 256
HOT = 10


def owned_ky():
    r = np.arange(ROWS)[:, None]
    b = np.arange(BULKS)[None, :]
    return np.where(b < BULKS // 2, 16 * b + r, 16 * (BULKS - 1 - b) + 8 + r).reshape(-1)


def split_table(a):
    a = np.asarray(a, np.float64)
    hi = a.astype(np.float32).astype(ml_dtypes.bfloat16)
    lo = (a - hi.astype(np.float64)).astype(np.float32).astype(ml_dtypes.bfloat16)
    return np.stack([hi, lo])


def tables():
    n = N
    ky = owned_ky()
    i = np.arange(n)
    turn = 2.0 * np.pi / n
    angle = turn * (ky[:, None] * i[None, :] % n)
    fwd = np.stack([np.cos(angle), -np.sin(angle)])
    inv = 2.0 * fwd
    zero = np.flatnonzero(ky == 0)[0]
    sign = np.where(i % 2 == 0, 1.0, -1.0)
    fwd[0, zero], fwd[1, zero] = 1.0, sign
    inv[0, zero], inv[1, zero] = 1.0, sign
    inv = inv / (n * n)
    angle = turn * (i[:, None] * i[None, :] % n)
    c, s = np.cos(angle), np.sin(angle)
    full = np.array([[c, -s], [s, c]])
    half = np.where(i[None, :] <= n // 2, c, s) * np.sqrt(2.0)
    half[:, 0], half[:, n // 2] = 1.0, sign
    none = np.zeros_like(half)
    packed = np.array([[half, none], [none, half]])
    both = []
    for m in (full, packed):
        m = m.transpose(0, 2, 1, 3).reshape(2, ROWS, n // ROWS, 2 * n)
        both.append(m.transpose(1, 0, 2, 3).reshape(2 * n, 2 * n))
    both = np.stack(both)
    mats = split_table(both).transpose(1, 0, 2, 3)
    mats_t = split_table(both.transpose(0, 2, 1)).transpose(1, 0, 2, 3)
    fwd = split_table(fwd.reshape(2 * DEVICES, n))
    inv_t = split_table(inv.transpose(0, 2, 1).reshape(2 * n, DEVICES))
    inv = split_table(inv.reshape(2, HALF, 2, n).transpose(2, 0, 1, 3).reshape(2, DEVICES, n))
    return fwd, mats, mats_t, inv, inv_t


def parts(x):
    hi = x.astype(jnp.bfloat16)
    lo = (x - hi.astype(jnp.float32)).astype(jnp.bfloat16)
    return hi, lo


def dot(a, b, dims=((1,), (0,))):
    return lax.dot_general(a, b, (dims, ((), ())), preferred_element_type=jnp.float32)


def dot3(ah, al, bh, bl, dims=((1,), (0,))):
    return dot(ah, bh, dims) + dot(ah, bl, dims) + dot(al, bh, dims)


def kernel(
    charge_h, fwd_h, shells_h, planes_h, green, mats, mats_t, inv, inv_t,
    out, electrodes,
    charge, fwd, shells, planes,
    sbuf, rbuf, obuf, home, mat, mat_t, inv_v, inv_t_v, g32, g_hi, g_lo, spec_ref, v_hi, v_lo, field_ref,
    lab, lab_src, lab_far, ebuf, erecv, eout, elrecv,
    gate, table_sem, ssem, rsem, hssem, hrsem, essem, ersem, elssem, elrsem, lssem, lrsem,
):
    r, b = lax.axis_index("row"), lax.axis_index("bulk")
    m = r * BULKS + b
    core = lax.rem(b, 2)
    pair = lax.div(m, 2)
    y, q0 = lax.div(pair, 32), lax.rem(pair, 32)
    first = m == 0
    feeder = m == BULKS // 2
    hot = lax.rem(b, HOT) == 0

    def at(d):
        return {"row": lax.div(d, BULKS), "bulk": lax.rem(d, BULKS)}

    def tile(ref, d):
        return ref.at[pl.ds(pl.multiple_of(d * 8, 8), 8), :]

    def push(src, dst, d, ss, rs):
        return pltpu.make_async_remote_copy(
            src_ref=src, dst_ref=dst, send_sem=ss, recv_sem=rs, device_id=at(d), device_id_type=MESH
        )

    def drain(ref, sem):
        pltpu.make_async_copy(ref, ref, sem).wait()

    which = jnp.where(first, 1, 0)
    moves = [
        (charge_h, charge), (fwd_h, fwd), (shells_h, shells), (planes_h, planes), (green, g32),
        (mats.at[which], mat), (mats_t.at[which], mat_t), (inv, inv_v), (inv_t, inv_t_v),
    ]
    loads = [pltpu.make_async_copy(src, dst, table_sem.at[i]) for i, (src, dst) in enumerate(moves)]
    for load in loads[:4]:
        load.start()

    barrier = pltpu.get_barrier_semaphore()
    z = lax.rem(r, 2) * 4 + lax.rem(lax.div(b, 2), 4)
    x = lax.div(b, 8)

    def place(px, py, pz, pc):
        return {"row": py * 2 + lax.div(pz, 4), "bulk": px * 8 + lax.rem(pz, 4) * 2 + pc}

    plane_peers = [place(lax.rem(x + i, 4), lax.rem(y + j, 4), z, core) for i in range(4) for j in range(4) if i + j]
    line_peers = [place(x, y, lax.rem(z + i, 8), lax.rem(core + j, 2)) for i in range(8) for j in range(2) if i + j]
    for peer in plane_peers + line_peers:
        pl.semaphore_signal(barrier, inc=1, device_id=peer, device_id_type=MESH)
    for load in loads[4:]:
        load.start()

    loads[0].wait()
    loads[1].wait()
    lane = lax.broadcasted_iota(jnp.int32, (DEVICES, 128), 1)
    for q in range(2):
        rows = jnp.concatenate([charge[:, 4 * q + j, :] for j in range(4)], axis=0)
        c_hi, c_lo = parts(rows)
        spec = dot3(fwd[0], fwd[1], c_hi, c_lo, ((1,), (1,)))
        for p in range(2):
            re = spec[:DEVICES, 128 * p : 128 * (p + 1)]
            im = spec[DEVICES:, 128 * p : 128 * (p + 1)]
            k = 4 * q + 2 * p
            sbuf[pl.ds(k, DEVICES, stride=8), :] = jnp.where(lane < 64, re, pltpu.roll(im, 64, 1))
            sbuf[pl.ds(k + 1, DEVICES, stride=8), :] = jnp.where(lane < 64, pltpu.roll(re, 64, 1), im)

    loads[2].wait()
    loads[3].wait()
    lab[:, :N] = shells[pl.ds(jnp.where(b < BULKS // 2, r, 8 - r), 1), :]
    lab_src[...] = shells[0:1, :]

    pl.semaphore_wait(barrier, len(plane_peers) + len(line_peers))
    for peer in line_peers:
        pl.semaphore_signal(gate, inc=1, device_id=peer, device_id_type=MESH)
    pl.semaphore_wait(gate, len(line_peers))

    pltpu.make_async_copy(tile(sbuf, m), tile(rbuf, m), rsem.at[y]).start()
    for c in range(2):

        @pl.when(core != c)
        def _(c=c):
            d = 2 * pair + c
            push(tile(sbuf, d), tile(rbuf, m), d, ssem, rsem.at[y]).start()

        def send(i, carry, c=c):
            t, j = lax.div(i, 32), lax.rem(i, 32)
            d = 2 * (lax.rem(y + t, 4) * 32 + lax.rem(q0 + j, 32)) + c
            push(tile(sbuf, d), tile(rbuf, m), d, ssem, rsem.at[y]).start()
            return carry

        lax.fori_loop(1, HALF, send, 0)

    @pl.when(feeder)
    def _():
        push(lab_src, lab_far, 0, lssem, lrsem).start()

    loads[4].wait()
    for s in range(8):
        hi, lo = parts(g32[s])
        g_hi[s] = hi
        g_lo[s] = lo
    loads[5].wait()
    loads[6].wait()

    @pl.when(feeder)
    def _():
        drain(lab_src, lssem)

    @pl.when(first)
    def _():
        drain(lab_far, lrsem)
        lab[:, N:] = lab_far[...]

    @pl.when(jnp.logical_not(first))
    def _():
        lab[:, N:] = lab[:, :N]

    spec_ref[...] = jnp.zeros_like(spec_ref)

    def gather(t, carry):
        g = lax.rem(y + 4 - t, 4)
        drain(rbuf.at[pl.ds(pl.multiple_of(g * 512, 512), 512), :], rsem.at[g])
        rows = [rbuf[pl.ds(pl.multiple_of(g * 512 + h * NZ, NZ), NZ), :] for h in range(2)]
        hi, lo = parts(jnp.concatenate(rows, axis=1))
        deep = pl.ds(pl.multiple_of(g * 256, 256), 256)
        spec_ref[...] += dot3(hi, lo, mat[0, deep, :], mat[1, deep, :])
        return carry

    lax.fori_loop(0, 4, gather, 0)

    def solve(t, carry):
        cols = pl.ds(pl.multiple_of(t * 256, 256), 256)
        s_hi, s_lo = parts(spec_ref[:, cols])
        label = lab[:, cols]
        acc = jnp.zeros((NZ, 256), jnp.float32)
        for s in range(8):
            mask = label == s
            m_hi = jnp.where(mask, s_hi, jnp.zeros_like(s_hi))
            m_lo = jnp.where(mask, s_lo, jnp.zeros_like(s_lo))
            acc = acc + dot3(g_hi[s], g_lo[s], m_hi, m_lo)
        hi, lo = parts(acc)
        v_hi[:, cols] = hi
        v_lo[:, cols] = lo
        return carry

    lax.fori_loop(0, 4, solve, 0)

    spot = core * HALF + pair
    for g in range(4):
        cols = slice(g * 256, (g + 1) * 256)
        back = dot3(v_hi[...], v_lo[...], mat_t[0, :, cols], mat_t[1, :, cols])
        for h in range(2):
            obuf[(2 * g + h) * NZ : (2 * g + h + 1) * NZ, :] = back[:, h * 128 : (h + 1) * 128]

    pltpu.make_async_copy(tile(obuf, m), tile(home, spot), hrsem.at[core]).start()

    def give(i, carry):
        d = lax.rem(m + i, DEVICES)
        push(tile(obuf, d), tile(home, spot), d, hssem, hrsem.at[core]).start()
        return carry

    lax.fori_loop(1, 32, give, 0)
    for g in range(ROWS):
        for p in range(4):
            ebuf[4 * g + p] = obuf[pl.ds(g * NZ + planes[p], 1), :]

    def plate(k, carry):
        d = lax.div(k, 4) * BULKS + HOT * lax.rem(k, 4)

        @pl.when(d != m)
        def _():
            push(ebuf.at[k], erecv.at[m], d, essem, ersem).start()

        @pl.when(d == m)
        def _():
            pltpu.make_async_copy(ebuf.at[k], erecv.at[m], ersem).start()

        return carry

    lax.fori_loop(0, 32, plate, 0)
    lax.fori_loop(32, DEVICES, give, 0)
    loads[7].wait()
    loads[8].wait()

    def regain(c):
        drain(home.at[pl.ds(c * 8 * HALF, 8 * HALF), :], hrsem.at[c])
        re, im = [], []
        for k in range(8):
            flip = jnp.transpose(home[pl.ds(c * 8 * HALF + k, HALF, stride=8), :])
            re.append(flip[:64])
            im.append(flip[64:])
        w_hi, w_lo = parts(jnp.concatenate([jnp.concatenate(re, axis=0), jnp.concatenate(im, axis=0)], axis=1))
        return dot3(w_hi, w_lo, inv_v[0, c], inv_v[1, c])

    field_ref[...] = regain(0)

    @pl.when(hot)
    def _():
        drain(erecv, ersem)
        e_hi, e_lo = parts(erecv[...].reshape(DEVICES, 128))
        both = dot3(inv_t_v[0], inv_t_v[1], e_hi, e_lo)
        eout[...] = both[:N] + pltpu.roll(both[N:], 64, 1)
        p = lax.div(b, HOT)

        def spread(j, c):
            d = r * BULKS + lax.rem(b + j, BULKS)
            src = eout.at[pl.ds(pl.multiple_of(lax.rem(d, BULKS) * 16, 16), 16), :]
            push(src, elrecv.at[p], d, elssem, elrsem).start()
            return c

        pltpu.make_async_copy(eout.at[pl.ds(pl.multiple_of(b * 16, 16), 16), :], elrecv.at[p], elrsem).start()
        lax.fori_loop(1, BULKS, spread, 0)

    rest = regain(1)
    for k in range(8):
        out[:, k, :] = field_ref[64 * k : 64 * (k + 1), :] + rest[64 * k : 64 * (k + 1)]

    drain(elrecv, elrsem)
    electrodes[...] = elrecv[:, :, :64]

    drain(sbuf.at[pl.ds(0, 8 * (DEVICES - 1)), :], ssem)
    drain(obuf.at[pl.ds(0, 8 * (DEVICES - 1)), :], hssem)
    drain(ebuf.at[pl.ds(0, 31)], essem)

    @pl.when(jnp.logical_not(hot))
    def _():
        drain(ebuf.at[0], essem)

    @pl.when(hot)
    def _():
        drain(eout.at[pl.ds(0, 16 * (BULKS - 1)), :], elssem)


def local(charge, green, shells, planes):
    fwd, mats, mats_t, inv, inv_t = (jnp.asarray(t) for t in tables())
    f32, bf16, i32 = jnp.float32, jnp.bfloat16, jnp.int32
    vmem, hbm = pl.BlockSpec(memory_space=pltpu.VMEM), pl.BlockSpec(memory_space=pltpu.HBM)
    dma = pltpu.SemaphoreType.DMA
    operands = (charge, fwd, shells, planes, green, mats, mats_t, inv, inv_t)
    field, plates = pl.pallas_call(
        kernel,
        out_shape=(
            jax.ShapeDtypeStruct(charge.shape, f32),
            jax.ShapeDtypeStruct((4, N // BULKS, N // ROWS), f32),
        ),
        in_specs=[hbm] * 9,
        out_specs=(vmem, vmem),
        scratch_shapes=[
            pltpu.VMEM(charge.shape, f32),
            pltpu.VMEM(fwd.shape, bf16),
            pltpu.VMEM(shells.shape, i32),
            pltpu.SMEM(planes.shape, i32),
            pltpu.VMEM((8 * DEVICES, 128), f32),
            pltpu.VMEM((8 * DEVICES, 128), f32),
            pltpu.VMEM((8 * DEVICES, 128), f32),
            pltpu.VMEM((8 * DEVICES, 128), f32),
            pltpu.VMEM(mats.shape[1:], bf16),
            pltpu.VMEM(mats.shape[1:], bf16),
            pltpu.VMEM(inv.shape, bf16),
            pltpu.VMEM(inv_t.shape, bf16),
            pltpu.VMEM((8, NZ, NZ), f32),
            pltpu.VMEM((8, NZ, NZ), bf16),
            pltpu.VMEM((8, NZ, NZ), bf16),
            pltpu.VMEM((NZ, 2 * N), f32),
            pltpu.VMEM((NZ, 2 * N), bf16),
            pltpu.VMEM((NZ, 2 * N), bf16),
            pltpu.VMEM((N, N), f32),
            pltpu.VMEM((1, 2 * N), i32),
            pltpu.VMEM((1, N), i32),
            pltpu.VMEM((1, N), i32),
            pltpu.VMEM((32, 1, 128), f32),
            pltpu.VMEM((DEVICES, 1, 128), f32),
            pltpu.VMEM((N, 128), f32),
            pltpu.VMEM((4, 16, 128), f32),
            pltpu.SemaphoreType.REGULAR,
            dma((9,)),
            dma,
            dma((4,)),
            dma,
            dma((2,)),
        ]
        + [dma] * 6,
        compiler_params=pltpu.CompilerParams(
            collective_id=0, has_side_effects=True, vmem_limit_bytes=48 * 1024 * 1024
        ),
    )(*(pltpu.with_memory_space_constraint(a, pltpu.HBM) for a in operands))
    return field, jnp.transpose(plates, (0, 2, 1))


def solution(mesh):
    placed = (P("row", "bulk", None), P(), P("bulk", None), P())
    return jax.shard_map(
        local,
        mesh=mesh,
        in_specs=placed,
        out_specs=(P("row", "bulk", None), P(None, "row", "bulk")),
        check_vma=False,
    )
```

```python
import functools

import jax
import jax.numpy as jnp
import ml_dtypes
import numpy as np
from jax import lax
from jax.experimental import pallas as pl
from jax.experimental.pallas import tpu as pltpu
from jax.sharding import PartitionSpec as P

MESH = pl.DeviceIdType.MESH
ROWS, BULKS = 8, 32
DEVICES = ROWS * BULKS
HALF = DEVICES // 2
N = 512
NZ = 256
HOT = 10


def owned_ky():
    r = np.arange(ROWS)[:, None]
    b = np.arange(BULKS)[None, :]
    return np.where(b < BULKS // 2, 16 * b + r, 16 * (BULKS - 1 - b) + 8 + r).reshape(-1)


def split_table(a):
    a = np.asarray(a, np.float64)
    hi = a.astype(np.float32).astype(ml_dtypes.bfloat16)
    lo = (a - hi.astype(np.float64)).astype(np.float32).astype(ml_dtypes.bfloat16)
    return np.stack([hi, lo])


def tables():
    n = N
    ky = owned_ky()
    i = np.arange(n)
    turn = 2.0 * np.pi / n
    angle = turn * (ky[:, None] * i[None, :] % n)
    fwd = np.stack([np.cos(angle), -np.sin(angle)])
    inv = 2.0 * fwd
    zero = np.flatnonzero(ky == 0)[0]
    sign = np.where(i % 2 == 0, 1.0, -1.0)
    fwd[0, zero], fwd[1, zero] = 1.0, sign
    inv[0, zero], inv[1, zero] = 1.0, sign
    inv = inv / (n * n)
    angle = turn * (i[:, None] * i[None, :] % n)
    c, s = np.cos(angle), np.sin(angle)
    full = np.array([[c, -s], [s, c]])
    half = np.where(i[None, :] <= n // 2, c, s) * np.sqrt(2.0)
    half[:, 0], half[:, n // 2] = 1.0, sign
    none = np.zeros_like(half)
    packed = np.array([[half, none], [none, half]])
    both = []
    for m in (full, packed):
        m = m.transpose(0, 2, 1, 3).reshape(2, ROWS, n // ROWS, 2 * n)
        both.append(m.transpose(1, 0, 2, 3).reshape(2 * n, 2 * n))
    both = np.stack(both)
    mats = split_table(both).transpose(1, 0, 2, 3)
    mats_t = split_table(both.transpose(0, 2, 1)).transpose(1, 0, 2, 3)
    fwd = split_table(fwd.reshape(2 * DEVICES, n))
    inv_t = split_table(inv.transpose(0, 2, 1).reshape(2 * n, DEVICES))
    inv = split_table(inv.reshape(2, HALF, 2, n).transpose(2, 0, 1, 3).reshape(2, DEVICES, n))
    return fwd, mats, mats_t, inv, inv_t


def parts(x):
    hi = x.astype(jnp.bfloat16)
    lo = (x - hi.astype(jnp.float32)).astype(jnp.bfloat16)
    return hi, lo


def dot(a, b, dims=((1,), (0,))):
    return lax.dot_general(a, b, (dims, ((), ())), preferred_element_type=jnp.float32)


def dot3(ah, al, bh, bl, dims=((1,), (0,))):
    return dot(ah, bh, dims) + dot(ah, bl, dims) + dot(al, bh, dims)


def kernel(
    charge_h, fwd_h, shells_h, planes_h, green, mats, mats_t, inv, inv_t,
    out, electrodes,
    charge, fwd, shells, planes,
    sbuf, rbuf, obuf, home, mat, mat_t, inv_v, inv_t_v, g32, g_hi, g_lo, spec_ref, v_hi, v_lo, field_ref,
    lab, lab_src, lab_far, ebuf, erecv, eout, elrecv,
    gate, table_sem, ssem, rsem, hssem, hrsem, essem, ersem, elssem, elrsem, lssem, lrsem,
):
    r, b = lax.axis_index("row"), lax.axis_index("bulk")
    m = r * BULKS + b
    core = lax.rem(b, 2)
    pair = lax.div(m, 2)
    y, q0 = lax.div(pair, 32), lax.rem(pair, 32)
    first = m == 0
    feeder = m == BULKS // 2
    hot = lax.rem(b, HOT) == 0

    def at(d):
        return {"row": lax.div(d, BULKS), "bulk": lax.rem(d, BULKS)}

    def tile(ref, d):
        return ref.at[pl.ds(pl.multiple_of(d * 8, 8), 8), :]

    def push(src, dst, d, ss, rs):
        return pltpu.make_async_remote_copy(
            src_ref=src, dst_ref=dst, send_sem=ss, recv_sem=rs, device_id=at(d), device_id_type=MESH
        )

    def drain(ref, sem):
        pltpu.make_async_copy(ref, ref, sem).wait()

    which = jnp.where(first, 1, 0)
    moves = [
        (charge_h, charge), (fwd_h, fwd), (shells_h, shells), (planes_h, planes), (green, g32),
        (mats.at[which], mat), (mats_t.at[which], mat_t), (inv, inv_v), (inv_t, inv_t_v),
    ]
    loads = [pltpu.make_async_copy(src, dst, table_sem.at[i]) for i, (src, dst) in enumerate(moves)]
    for load in loads[:4]:
        load.start()

    barrier = pltpu.get_barrier_semaphore()
    z = lax.rem(r, 2) * 4 + lax.rem(lax.div(b, 2), 4)
    x = lax.div(b, 8)

    def place(px, py, pz, pc):
        return (py * 2 + lax.div(pz, 4)) * BULKS + px * 8 + lax.rem(pz, 4) * 2 + pc

    plane_peers = [place(lax.rem(x + i, 4), lax.rem(y + j, 4), z, core) for i in range(4) for j in range(4) if i + j]
    line_peers = [place(x, y, lax.rem(z + i, 8), lax.rem(core + j, 2)) for i in range(8) for j in range(2) if i + j]
    for peer in plane_peers + line_peers:
        pl.semaphore_signal(barrier, inc=1, device_id=at(peer), device_id_type=MESH)
    for load in loads[4:]:
        load.start()

    loads[0].wait()
    loads[1].wait()
    lane = lax.broadcasted_iota(jnp.int32, (DEVICES, 128), 1)
    for q in range(2):
        if q == 1:
            pl.semaphore_wait(barrier, len(plane_peers) + len(line_peers))
            for peer in line_peers:
                pl.semaphore_signal(gate, inc=1, device_id=at(peer), device_id_type=MESH)
        rows = jnp.concatenate([charge[:, 4 * q + j, :] for j in range(4)], axis=0)
        c_hi, c_lo = parts(rows)
        spec = dot3(fwd[0], fwd[1], c_hi, c_lo, ((1,), (1,)))
        for p in range(2):
            re = spec[:DEVICES, 128 * p : 128 * (p + 1)]
            im = spec[DEVICES:, 128 * p : 128 * (p + 1)]
            k = 4 * q + 2 * p
            sbuf[pl.ds(k, DEVICES, stride=8), :] = jnp.where(lane < 64, re, pltpu.roll(im, 64, 1))
            sbuf[pl.ds(k + 1, DEVICES, stride=8), :] = jnp.where(lane < 64, pltpu.roll(re, 64, 1), im)

    loads[2].wait()
    loads[3].wait()
    lab[:, :N] = shells[pl.ds(jnp.where(b < BULKS // 2, r, 8 - r), 1), :]
    lab_src[...] = shells[0:1, :]

    pltpu.make_async_copy(tile(sbuf, m), tile(rbuf, m), rsem.at[y]).start()

    def send(d):
        push(tile(sbuf, d), tile(rbuf, m), d, ssem, rsem.at[y]).start()

    for peer in line_peers + plane_peers:
        send(peer)
    pl.semaphore_wait(gate, len(line_peers))
    for c in range(2):
        def across(k, carry, c=c):
            base = lax.rem(y + lax.div(k, 4), 4) * 2 * BULKS + lax.rem(x + lax.rem(k, 4), 4) * 8 + c

            def along(j, inner):
                pz = lax.rem(z + j, 8)
                send(base + lax.div(pz, 4) * BULKS + lax.rem(pz, 4) * 2)
                return inner

            return lax.fori_loop(jnp.where(core == c, 1, 0), 8, along, carry)

        lax.fori_loop(1, 16, across, 0)

    @pl.when(feeder)
    def _():
        push(lab_src, lab_far, 0, lssem, lrsem).start()

    loads[4].wait()
    for s in range(8):
        hi, lo = parts(g32[s])
        g_hi[s] = hi
        g_lo[s] = lo
    loads[5].wait()
    loads[6].wait()

    @pl.when(feeder)
    def _():
        drain(lab_src, lssem)

    @pl.when(first)
    def _():
        drain(lab_far, lrsem)
        lab[:, N:] = lab_far[...]

    @pl.when(jnp.logical_not(first))
    def _():
        lab[:, N:] = lab[:, :N]

    spec_ref[...] = jnp.zeros_like(spec_ref)

    def gather(t, carry):
        g = lax.rem(y + 4 - t, 4)
        drain(rbuf.at[pl.ds(pl.multiple_of(g * 512, 512), 512), :], rsem.at[g])
        rows = [rbuf[pl.ds(pl.multiple_of(g * 512 + h * NZ, NZ), NZ), :] for h in range(2)]
        hi, lo = parts(jnp.concatenate(rows, axis=1))
        deep = pl.ds(pl.multiple_of(g * 256, 256), 256)
        spec_ref[...] += dot3(hi, lo, mat[0, deep, :], mat[1, deep, :])
        return carry

    lax.fori_loop(0, 4, gather, 0)

    def solve(t, carry):
        cols = pl.ds(pl.multiple_of(t * 256, 256), 256)
        s_hi, s_lo = parts(spec_ref[:, cols])
        label = lab[:, cols]
        acc = jnp.zeros((NZ, 256), jnp.float32)
        for s in range(8):
            mask = label == s
            m_hi = jnp.where(mask, s_hi, jnp.zeros_like(s_hi))
            m_lo = jnp.where(mask, s_lo, jnp.zeros_like(s_lo))
            acc = acc + dot3(g_hi[s], g_lo[s], m_hi, m_lo)
        hi, lo = parts(acc)
        v_hi[:, cols] = hi
        v_lo[:, cols] = lo
        return carry

    lax.fori_loop(0, 4, solve, 0)

    spot = core * HALF + pair
    for g in range(4):
        cols = slice(g * 256, (g + 1) * 256)
        back = dot3(v_hi[...], v_lo[...], mat_t[0, :, cols], mat_t[1, :, cols])
        for h in range(2):
            obuf[(2 * g + h) * NZ : (2 * g + h + 1) * NZ, :] = back[:, h * 128 : (h + 1) * 128]

    pltpu.make_async_copy(tile(obuf, m), tile(home, spot), hrsem.at[core]).start()

    def give(i, carry):
        d = lax.rem(m + i, DEVICES)
        push(tile(obuf, d), tile(home, spot), d, hssem, hrsem.at[core]).start()
        return carry

    lax.fori_loop(1, 32, give, 0)
    for g in range(ROWS):
        for p in range(4):
            ebuf[4 * g + p] = obuf[pl.ds(g * NZ + planes[p], 1), :]

    def plate(k, carry):
        d = lax.div(k, 4) * BULKS + HOT * lax.rem(k, 4)

        @pl.when(d != m)
        def _():
            push(ebuf.at[k], erecv.at[m], d, essem, ersem).start()

        @pl.when(d == m)
        def _():
            pltpu.make_async_copy(ebuf.at[k], erecv.at[m], ersem).start()

        return carry

    lax.fori_loop(0, 32, plate, 0)
    lax.fori_loop(32, DEVICES, give, 0)
    loads[7].wait()
    loads[8].wait()

    def regain(c):
        drain(home.at[pl.ds(c * 8 * HALF, 8 * HALF), :], hrsem.at[c])
        re, im = [], []
        for k in range(8):
            flip = jnp.transpose(home[pl.ds(c * 8 * HALF + k, HALF, stride=8), :])
            re.append(flip[:64])
            im.append(flip[64:])
        w_hi, w_lo = parts(jnp.concatenate([jnp.concatenate(re, axis=0), jnp.concatenate(im, axis=0)], axis=1))
        return dot3(w_hi, w_lo, inv_v[0, c], inv_v[1, c])

    field_ref[...] = regain(0)

    @pl.when(hot)
    def _():
        drain(erecv, ersem)
        e_hi, e_lo = parts(erecv[...].reshape(DEVICES, 128))
        both = dot3(inv_t_v[0], inv_t_v[1], e_hi, e_lo)
        near = (both[:N] + pltpu.roll(both[N:], 64, 1)).reshape(BULKS, 16, 128)
        far = (pltpu.roll(both[:N], 64, 1) + both[N:]).reshape(BULKS, 16, 128)
        side = lax.broadcasted_iota(jnp.int32, (BULKS, 8, 128), 2)
        eout[...] = jnp.where(side < 64, near[:, :8], far[:, 8:]).reshape(8 * BULKS, 128)
        p = lax.div(b, HOT)

        def spread(j, c):
            d = r * BULKS + lax.rem(b + j, BULKS)
            push(tile(eout, lax.rem(d, BULKS)), elrecv.at[p], d, elssem, elrsem).start()
            return c

        pltpu.make_async_copy(tile(eout, b), elrecv.at[p], elrsem).start()
        lax.fori_loop(1, BULKS, spread, 0)

    rest = regain(1)
    for k in range(8):
        out[:, k, :] = field_ref[64 * k : 64 * (k + 1), :] + rest[64 * k : 64 * (k + 1)]

    drain(elrecv, elrsem)
    electrodes[:, :8, :] = elrecv[:, :, :64]
    electrodes[:, 8:, :] = elrecv[:, :, 64:]

    drain(sbuf.at[pl.ds(0, 8 * (DEVICES - 1)), :], ssem)
    drain(obuf.at[pl.ds(0, 8 * (DEVICES - 1)), :], hssem)
    drain(ebuf.at[pl.ds(0, 31)], essem)

    @pl.when(jnp.logical_not(hot))
    def _():
        drain(ebuf.at[0], essem)

    @pl.when(hot)
    def _():
        drain(eout.at[pl.ds(0, 8 * (BULKS - 1)), :], elssem)


def local(charge, green, shells, planes):
    fwd, mats, mats_t, inv, inv_t = (jnp.asarray(t) for t in tables())
    f32, bf16, i32 = jnp.float32, jnp.bfloat16, jnp.int32
    vmem, hbm = pl.BlockSpec(memory_space=pltpu.VMEM), pl.BlockSpec(memory_space=pltpu.HBM)
    dma = pltpu.SemaphoreType.DMA
    operands = (charge, fwd, shells, planes, green, mats, mats_t, inv, inv_t)
    field, plates = pl.pallas_call(
        kernel,
        out_shape=(
            jax.ShapeDtypeStruct(charge.shape, f32),
            jax.ShapeDtypeStruct((4, N // BULKS, N // ROWS), f32),
        ),
        in_specs=[hbm] * 9,
        out_specs=(vmem, vmem),
        scratch_shapes=[
            pltpu.VMEM(charge.shape, f32),
            pltpu.VMEM(fwd.shape, bf16),
            pltpu.VMEM(shells.shape, i32),
            pltpu.SMEM(planes.shape, i32),
            pltpu.VMEM((8 * DEVICES, 128), f32),
            pltpu.VMEM((8 * DEVICES, 128), f32),
            pltpu.VMEM((8 * DEVICES, 128), f32),
            pltpu.VMEM((8 * DEVICES, 128), f32),
            pltpu.VMEM(mats.shape[1:], bf16),
            pltpu.VMEM(mats.shape[1:], bf16),
            pltpu.VMEM(inv.shape, bf16),
            pltpu.VMEM(inv_t.shape, bf16),
            pltpu.VMEM((8, NZ, NZ), f32),
            pltpu.VMEM((8, NZ, NZ), bf16),
            pltpu.VMEM((8, NZ, NZ), bf16),
            pltpu.VMEM((NZ, 2 * N), f32),
            pltpu.VMEM((NZ, 2 * N), bf16),
            pltpu.VMEM((NZ, 2 * N), bf16),
            pltpu.VMEM((N, N), f32),
            pltpu.VMEM((1, 2 * N), i32),
            pltpu.VMEM((1, N), i32),
            pltpu.VMEM((1, N), i32),
            pltpu.VMEM((32, 1, 128), f32),
            pltpu.VMEM((DEVICES, 1, 128), f32),
            pltpu.VMEM((8 * BULKS, 128), f32),
            pltpu.VMEM((4, 8, 128), f32),
            pltpu.SemaphoreType.REGULAR,
            dma((9,)),
            dma,
            dma((4,)),
            dma,
            dma((2,)),
        ]
        + [dma] * 6,
        compiler_params=pltpu.CompilerParams(
            collective_id=0, has_side_effects=True, vmem_limit_bytes=48 * 1024 * 1024
        ),
    )(*(pltpu.with_memory_space_constraint(a, pltpu.HBM) for a in operands))
    return field, jnp.transpose(plates, (0, 2, 1))


def solution(mesh):
    placed = (P("row", "bulk", None), P(), P("bulk", None), P())
    return jax.shard_map(
        local,
        mesh=mesh,
        in_specs=placed,
        out_specs=(P("row", "bulk", None), P(None, "row", "bulk")),
        check_vma=False,
    )
```

```python
import functools

import jax
import jax.numpy as jnp
import ml_dtypes
import numpy as np
from jax import lax
from jax.experimental import pallas as pl
from jax.experimental.pallas import tpu as pltpu
from jax.sharding import PartitionSpec as P

MESH = pl.DeviceIdType.MESH
ROWS, BULKS = 8, 32
DEVICES = ROWS * BULKS
HALF = DEVICES // 2
N = 512
NZ = 256
HOT = 10


def owned_ky():
    r = np.arange(ROWS)[:, None]
    b = np.arange(BULKS)[None, :]
    return np.where(b < BULKS // 2, 16 * b + r, 16 * (BULKS - 1 - b) + 8 + r).reshape(-1)


def split_table(a):
    a = np.asarray(a, np.float64)
    hi = a.astype(np.float32).astype(ml_dtypes.bfloat16)
    lo = (a - hi.astype(np.float64)).astype(np.float32).astype(ml_dtypes.bfloat16)
    return np.stack([hi, lo])


def tables():
    n = N
    ky = owned_ky()
    i = np.arange(n)
    turn = 2.0 * np.pi / n
    angle = turn * (ky[:, None] * i[None, :] % n)
    fwd = np.stack([np.cos(angle), -np.sin(angle)])
    inv = 2.0 * fwd
    zero = np.flatnonzero(ky == 0)[0]
    sign = np.where(i % 2 == 0, 1.0, -1.0)
    fwd[0, zero], fwd[1, zero] = 1.0, sign
    inv[0, zero], inv[1, zero] = 1.0, sign
    inv = inv / (n * n)
    angle = turn * (i[:, None] * i[None, :] % n)
    c, s = np.cos(angle), np.sin(angle)
    full = np.array([[c, -s], [s, c]])
    half = np.where(i[None, :] <= n // 2, c, s) * np.sqrt(2.0)
    half[:, 0], half[:, n // 2] = 1.0, sign
    none = np.zeros_like(half)
    packed = np.array([[half, none], [none, half]])
    both = []
    for m in (full, packed):
        m = m.transpose(0, 2, 1, 3).reshape(2, ROWS, n // ROWS, 2 * n)
        both.append(m.transpose(1, 0, 2, 3).reshape(2 * n, 2 * n))
    both = np.stack(both)
    mats = split_table(both).transpose(1, 0, 2, 3)
    mats_t = split_table(both.transpose(0, 2, 1)).transpose(1, 0, 2, 3)
    fwd = split_table(fwd.reshape(2 * DEVICES, n))
    inv_t = split_table(inv.transpose(0, 2, 1).reshape(2 * n, DEVICES))
    inv = split_table(inv.reshape(2, HALF, 2, n).transpose(2, 0, 1, 3).reshape(2, DEVICES, n))
    return fwd, mats, mats_t, inv, inv_t


def parts(x):
    hi = x.astype(jnp.bfloat16)
    lo = (x - hi.astype(jnp.float32)).astype(jnp.bfloat16)
    return hi, lo


def dot(a, b, dims=((1,), (0,))):
    return lax.dot_general(a, b, (dims, ((), ())), preferred_element_type=jnp.float32)


def dot3(ah, al, bh, bl, dims=((1,), (0,))):
    return dot(ah, bh, dims) + dot(ah, bl, dims) + dot(al, bh, dims)


def kernel(
    charge_h, fwd_h, shells_h, planes_h, green, mats, mats_t, inv, inv_t,
    out, electrodes,
    charge, fwd, shells, planes,
    sbuf, rbuf, obuf, home, mat, mat_t, inv_v, inv_t_v, g32, g_hi, g_lo, spec_ref, v_hi, v_lo, field_ref,
    lab, lab_src, lab_far, ebuf, erecv, eout, elrecv,
    gate, table_sem, ssem, rsem, hssem, hrsem, essem, ersem, elssem, elrsem, lssem, lrsem,
):
    r, b = lax.axis_index("row"), lax.axis_index("bulk")
    m = r * BULKS + b
    core = lax.rem(b, 2)
    pair = lax.div(m, 2)
    y, q0 = lax.div(pair, 32), lax.rem(pair, 32)
    first = m == 0
    feeder = m == BULKS // 2
    hot = lax.rem(b, HOT) == 0

    def at(d):
        return {"row": lax.div(d, BULKS), "bulk": lax.rem(d, BULKS)}

    def tile(ref, d):
        return ref.at[pl.ds(pl.multiple_of(d * 8, 8), 8), :]

    def push(src, dst, d, ss, rs):
        return pltpu.make_async_remote_copy(
            src_ref=src, dst_ref=dst, send_sem=ss, recv_sem=rs, device_id=at(d), device_id_type=MESH
        )

    def drain(ref, sem):
        pltpu.make_async_copy(ref, ref, sem).wait()

    which = jnp.where(first, 1, 0)
    moves = [
        (charge_h, charge), (fwd_h, fwd), (shells_h, shells), (planes_h, planes), (green, g32),
        (mats.at[which], mat), (mats_t.at[which], mat_t), (inv, inv_v), (inv_t, inv_t_v),
    ]
    loads = [pltpu.make_async_copy(src, dst, table_sem.at[i]) for i, (src, dst) in enumerate(moves)]
    for load in loads[:4]:
        load.start()

    barrier = pltpu.get_barrier_semaphore()
    z = lax.rem(r, 2) * 4 + lax.rem(lax.div(b, 2), 4)
    x = lax.div(b, 8)

    def place(px, py, pz, pc):
        return (py * 2 + lax.div(pz, 4)) * BULKS + px * 8 + lax.rem(pz, 4) * 2 + pc

    plane_peers = [place(lax.rem(x + i, 4), lax.rem(y + j, 4), z, core) for i in range(4) for j in range(4) if i + j]
    line_peers = [place(x, y, lax.rem(z + i, 8), lax.rem(core + j, 2)) for i in range(8) for j in range(2) if i + j]
    for peer in plane_peers + line_peers:
        pl.semaphore_signal(barrier, inc=1, device_id=at(peer), device_id_type=MESH)
    for load in loads[4:]:
        load.start()

    loads[0].wait()
    loads[1].wait()
    lane = lax.broadcasted_iota(jnp.int32, (DEVICES, 128), 1)
    for q in range(2):
        rows = jnp.concatenate([charge[:, 4 * q + j, :] for j in range(4)], axis=0)
        c_hi, c_lo = parts(rows)
        spec = dot3(fwd[0], fwd[1], c_hi, c_lo, ((1,), (1,)))
        if q == 1:
            pl.semaphore_wait(barrier, len(plane_peers) + len(line_peers))
            for peer in line_peers:
                pl.semaphore_signal(gate, inc=1, device_id=at(peer), device_id_type=MESH)
        for p in range(2):
            re = spec[:DEVICES, 128 * p : 128 * (p + 1)]
            im = spec[DEVICES:, 128 * p : 128 * (p + 1)]
            k = 4 * q + 2 * p
            sbuf[pl.ds(k, DEVICES, stride=8), :] = jnp.where(lane < 64, re, pltpu.roll(im, 64, 1))
            sbuf[pl.ds(k + 1, DEVICES, stride=8), :] = jnp.where(lane < 64, pltpu.roll(re, 64, 1), im)

    loads[2].wait()
    loads[3].wait()
    lab[:, :N] = shells[pl.ds(jnp.where(b < BULKS // 2, r, 8 - r), 1), :]
    lab_src[...] = shells[0:1, :]

    pltpu.make_async_copy(tile(sbuf, m), tile(rbuf, m), rsem.at[y]).start()

    def send(d):
        push(tile(sbuf, d), tile(rbuf, m), d, ssem, rsem.at[y]).start()

    for peer in line_peers + plane_peers:
        send(peer)
    pl.semaphore_wait(gate, len(line_peers))
    for c in range(2):
        def across(k, carry, c=c):
            base = lax.rem(y + lax.div(k, 4), 4) * 2 * BULKS + lax.rem(x + lax.rem(k, 4), 4) * 8 + c

            def along(j, inner):
                pz = lax.rem(z + j, 8)
                send(base + lax.div(pz, 4) * BULKS + lax.rem(pz, 4) * 2)
                return inner

            return lax.fori_loop(jnp.where(core == c, 1, 0), 8, along, carry)

        lax.fori_loop(1, 16, across, 0)

    @pl.when(feeder)
    def _():
        push(lab_src, lab_far, 0, lssem, lrsem).start()

    loads[4].wait()
    for s in range(8):
        hi, lo = parts(g32[s])
        g_hi[s] = hi
        g_lo[s] = lo
    loads[5].wait()
    loads[6].wait()

    @pl.when(feeder)
    def _():
        drain(lab_src, lssem)

    @pl.when(first)
    def _():
        drain(lab_far, lrsem)
        lab[:, N:] = lab_far[...]

    @pl.when(jnp.logical_not(first))
    def _():
        lab[:, N:] = lab[:, :N]

    spec_ref[...] = jnp.zeros_like(spec_ref)

    def gather(t, carry):
        g = lax.rem(y + 4 - t, 4)
        drain(rbuf.at[pl.ds(pl.multiple_of(g * 512, 512), 512), :], rsem.at[g])
        rows = [rbuf[pl.ds(pl.multiple_of(g * 512 + h * NZ, NZ), NZ), :] for h in range(2)]
        hi, lo = parts(jnp.concatenate(rows, axis=1))
        deep = pl.ds(pl.multiple_of(g * 256, 256), 256)
        spec_ref[...] += dot3(hi, lo, mat[0, deep, :], mat[1, deep, :])
        return carry

    lax.fori_loop(0, 4, gather, 0, unroll=True)

    def solve(t, carry):
        cols = pl.ds(pl.multiple_of(t * 256, 256), 256)
        s_hi, s_lo = parts(spec_ref[:, cols])
        label = lab[:, cols]
        acc = jnp.zeros((NZ, 256), jnp.float32)
        for s in range(8):
            mask = label == s
            m_hi = jnp.where(mask, s_hi, jnp.zeros_like(s_hi))
            m_lo = jnp.where(mask, s_lo, jnp.zeros_like(s_lo))
            acc = acc + dot3(g_hi[s], g_lo[s], m_hi, m_lo)
        hi, lo = parts(acc)
        v_hi[:, cols] = hi
        v_lo[:, cols] = lo
        return carry

    lax.fori_loop(0, 4, solve, 0, unroll=True)

    spot = core * HALF + pair
    for g in range(4):
        cols = slice(g * 256, (g + 1) * 256)
        back = dot3(v_hi[...], v_lo[...], mat_t[0, :, cols], mat_t[1, :, cols])
        for h in range(2):
            obuf[(2 * g + h) * NZ : (2 * g + h + 1) * NZ, :] = back[:, h * 128 : (h + 1) * 128]

    pltpu.make_async_copy(tile(obuf, m), tile(home, spot), hrsem.at[core]).start()

    def give(i, carry):
        d = lax.rem(m + i, DEVICES)
        push(tile(obuf, d), tile(home, spot), d, hssem, hrsem.at[core]).start()
        return carry

    lax.fori_loop(1, 32, give, 0)
    for g in range(ROWS):
        for p in range(4):
            ebuf[4 * g + p] = obuf[pl.ds(g * NZ + planes[p], 1), :]

    def plate(k, carry):
        d = lax.div(k, 4) * BULKS + HOT * lax.rem(k, 4)

        @pl.when(d != m)
        def _():
            push(ebuf.at[k], erecv.at[m], d, essem, ersem).start()

        @pl.when(d == m)
        def _():
            pltpu.make_async_copy(ebuf.at[k], erecv.at[m], ersem).start()

        return carry

    lax.fori_loop(0, 32, plate, 0)
    lax.fori_loop(32, DEVICES, give, 0)
    loads[7].wait()
    loads[8].wait()

    def regain(c):
        drain(home.at[pl.ds(c * 8 * HALF, 8 * HALF), :], hrsem.at[c])
        re, im = [], []
        for k in range(8):
            flip = jnp.transpose(home[pl.ds(c * 8 * HALF + k, HALF, stride=8), :])
            re.append(flip[:64])
            im.append(flip[64:])
        w_hi, w_lo = parts(jnp.concatenate([jnp.concatenate(re, axis=0), jnp.concatenate(im, axis=0)], axis=1))
        return dot3(w_hi, w_lo, inv_v[0, c], inv_v[1, c])

    field_ref[...] = regain(0)

    @pl.when(hot)
    def _():
        drain(erecv, ersem)
        e_hi, e_lo = parts(erecv[...].reshape(DEVICES, 128))
        both = dot3(inv_t_v[0], inv_t_v[1], e_hi, e_lo)
        near = (both[:N] + pltpu.roll(both[N:], 64, 1)).reshape(BULKS, 16, 128)
        far = (pltpu.roll(both[:N], 64, 1) + both[N:]).reshape(BULKS, 16, 128)
        side = lax.broadcasted_iota(jnp.int32, (BULKS, 8, 128), 2)
        eout[...] = jnp.where(side < 64, near[:, :8], far[:, 8:]).reshape(8 * BULKS, 128)
        p = lax.div(b, HOT)

        def spread(j, c):
            d = r * BULKS + lax.rem(b + j, BULKS)
            push(tile(eout, lax.rem(d, BULKS)), elrecv.at[p], d, elssem, elrsem).start()
            return c

        pltpu.make_async_copy(tile(eout, b), elrecv.at[p], elrsem).start()
        lax.fori_loop(1, BULKS, spread, 0)

    rest = regain(1)
    for k in range(8):
        out[:, k, :] = field_ref[64 * k : 64 * (k + 1), :] + rest[64 * k : 64 * (k + 1)]

    drain(elrecv, elrsem)
    electrodes[:, :8, :] = elrecv[:, :, :64]
    electrodes[:, 8:, :] = elrecv[:, :, 64:]

    drain(sbuf.at[pl.ds(0, 8 * (DEVICES - 1)), :], ssem)
    drain(obuf.at[pl.ds(0, 8 * (DEVICES - 1)), :], hssem)
    drain(ebuf.at[pl.ds(0, 31)], essem)

    @pl.when(jnp.logical_not(hot))
    def _():
        drain(ebuf.at[0], essem)

    @pl.when(hot)
    def _():
        drain(eout.at[pl.ds(0, 8 * (BULKS - 1)), :], elssem)


def local(charge, green, shells, planes):
    fwd, mats, mats_t, inv, inv_t = (jnp.asarray(t) for t in tables())
    f32, bf16, i32 = jnp.float32, jnp.bfloat16, jnp.int32
    vmem, hbm = pl.BlockSpec(memory_space=pltpu.VMEM), pl.BlockSpec(memory_space=pltpu.HBM)
    dma = pltpu.SemaphoreType.DMA
    operands = (charge, fwd, shells, planes, green, mats, mats_t, inv, inv_t)
    field, plates = pl.pallas_call(
        kernel,
        out_shape=(
            jax.ShapeDtypeStruct(charge.shape, f32),
            jax.ShapeDtypeStruct((4, N // BULKS, N // ROWS), f32),
        ),
        in_specs=[hbm] * 9,
        out_specs=(vmem, vmem),
        scratch_shapes=[
            pltpu.VMEM(charge.shape, f32),
            pltpu.VMEM(fwd.shape, bf16),
            pltpu.VMEM(shells.shape, i32),
            pltpu.SMEM(planes.shape, i32),
            pltpu.VMEM((8 * DEVICES, 128), f32),
            pltpu.VMEM((8 * DEVICES, 128), f32),
            pltpu.VMEM((8 * DEVICES, 128), f32),
            pltpu.VMEM((8 * DEVICES, 128), f32),
            pltpu.VMEM(mats.shape[1:], bf16),
            pltpu.VMEM(mats.shape[1:], bf16),
            pltpu.VMEM(inv.shape, bf16),
            pltpu.VMEM(inv_t.shape, bf16),
            pltpu.VMEM((8, NZ, NZ), f32),
            pltpu.VMEM((8, NZ, NZ), bf16),
            pltpu.VMEM((8, NZ, NZ), bf16),
            pltpu.VMEM((NZ, 2 * N), f32),
            pltpu.VMEM((NZ, 2 * N), bf16),
            pltpu.VMEM((NZ, 2 * N), bf16),
            pltpu.VMEM((N, N), f32),
            pltpu.VMEM((1, 2 * N), i32),
            pltpu.VMEM((1, N), i32),
            pltpu.VMEM((1, N), i32),
            pltpu.VMEM((32, 1, 128), f32),
            pltpu.VMEM((DEVICES, 1, 128), f32),
            pltpu.VMEM((8 * BULKS, 128), f32),
            pltpu.VMEM((4, 8, 128), f32),
            pltpu.SemaphoreType.REGULAR,
            dma((9,)),
            dma,
            dma((4,)),
            dma,
            dma((2,)),
        ]
        + [dma] * 6,
        compiler_params=pltpu.CompilerParams(
            collective_id=0, has_side_effects=True, vmem_limit_bytes=48 * 1024 * 1024
        ),
    )(*(pltpu.with_memory_space_constraint(a, pltpu.HBM) for a in operands))
    return field, jnp.transpose(plates, (0, 2, 1))


def solution(mesh):
    placed = (P("row", "bulk", None), P(), P("bulk", None), P())
    return jax.shard_map(
        local,
        mesh=mesh,
        in_specs=placed,
        out_specs=(P("row", "bulk", None), P(None, "row", "bulk")),
        check_vma=False,
    )
```

```python
import functools

import jax
import jax.numpy as jnp
import ml_dtypes
import numpy as np
from jax import lax
from jax.experimental import pallas as pl
from jax.experimental.pallas import tpu as pltpu
from jax.sharding import PartitionSpec as P

MESH = pl.DeviceIdType.MESH
ROWS, BULKS = 8, 32
DEVICES = ROWS * BULKS
HALF = DEVICES // 2
N = 512
NZ = 256
HOT = 10


def owned_ky():
    r = np.arange(ROWS)[:, None]
    b = np.arange(BULKS)[None, :]
    return np.where(b < BULKS // 2, 16 * b + r, 16 * (BULKS - 1 - b) + 8 + r).reshape(-1)


def split_table(a):
    a = np.asarray(a, np.float64)
    hi = a.astype(np.float32).astype(ml_dtypes.bfloat16)
    lo = (a - hi.astype(np.float64)).astype(np.float32).astype(ml_dtypes.bfloat16)
    return np.stack([hi, lo])


def tables():
    n = N
    ky = owned_ky()
    i = np.arange(n)
    turn = 2.0 * np.pi / n
    angle = turn * (ky[:, None] * i[None, :] % n)
    fwd = np.stack([np.cos(angle), -np.sin(angle)])
    inv = 2.0 * fwd
    zero = np.flatnonzero(ky == 0)[0]
    sign = np.where(i % 2 == 0, 1.0, -1.0)
    fwd[0, zero], fwd[1, zero] = 1.0, sign
    inv[0, zero], inv[1, zero] = 1.0, sign
    inv = inv / (n * n)
    angle = turn * (i[:, None] * i[None, :] % n)
    c, s = np.cos(angle), np.sin(angle)
    full = np.array([[c, -s], [s, c]])
    half = np.where(i[None, :] <= n // 2, c, s) * np.sqrt(2.0)
    half[:, 0], half[:, n // 2] = 1.0, sign
    none = np.zeros_like(half)
    packed = np.array([[half, none], [none, half]])
    both = []
    for m in (full, packed):
        m = m.transpose(0, 2, 1, 3).reshape(2, ROWS, n // ROWS, 2 * n)
        both.append(m.transpose(1, 0, 2, 3).reshape(2 * n, 2 * n))
    both = np.stack(both)
    mats = split_table(both).transpose(1, 0, 2, 3)
    mats_t = split_table(both.transpose(0, 2, 1)).transpose(1, 0, 2, 3)
    fwd = split_table(fwd.reshape(2 * DEVICES, n))
    inv_t = split_table(inv.transpose(0, 2, 1).reshape(2 * n, DEVICES))
    inv = split_table(inv.reshape(2, HALF, 2, n).transpose(2, 0, 1, 3).reshape(2, DEVICES, n))
    return fwd, mats, mats_t, inv, inv_t


def parts(x):
    hi = x.astype(jnp.bfloat16)
    lo = (x - hi.astype(jnp.float32)).astype(jnp.bfloat16)
    return hi, lo


def dot(a, b, dims=((1,), (0,))):
    return lax.dot_general(a, b, (dims, ((), ())), preferred_element_type=jnp.float32)


def dot3(ah, al, bh, bl, dims=((1,), (0,))):
    return dot(ah, bh, dims) + dot(ah, bl, dims) + dot(al, bh, dims)


def kernel(
    charge_h, fwd_h, shells_h, planes_h, green, mats, mats_t, inv, inv_t,
    out, electrodes,
    charge, fwd, shells, planes,
    sbuf, rbuf, obuf, home, mat, mat_t, inv_v, inv_t_v, g32, g_hi, g_lo, spec_ref, v_hi, v_lo, field_ref,
    lab, lab_src, lab_far, ebuf, erecv, eout, elrecv,
    gate, table_sem, ssem, rsem, hssem, hrsem, essem, ersem, elssem, elrsem, lssem, lrsem,
):
    r, b = lax.axis_index("row"), lax.axis_index("bulk")
    m = r * BULKS + b
    core = lax.rem(b, 2)
    pair = lax.div(m, 2)
    y, q0 = lax.div(pair, 32), lax.rem(pair, 32)
    first = m == 0
    feeder = m == BULKS // 2
    hot = lax.rem(b, HOT) == 0

    def at(d):
        return {"row": lax.div(d, BULKS), "bulk": lax.rem(d, BULKS)}

    def tile(ref, d):
        return ref.at[pl.ds(pl.multiple_of(d * 8, 8), 8), :]

    def push(src, dst, d, ss, rs):
        return pltpu.make_async_remote_copy(
            src_ref=src, dst_ref=dst, send_sem=ss, recv_sem=rs, device_id=at(d), device_id_type=MESH
        )

    def drain(ref, sem):
        pltpu.make_async_copy(ref, ref, sem).wait()

    which = jnp.where(first, 1, 0)
    moves = [
        (charge_h, charge), (fwd_h, fwd), (shells_h, shells), (planes_h, planes), (green, g32),
        (mats.at[which], mat), (mats_t.at[which], mat_t), (inv, inv_v), (inv_t, inv_t_v),
    ]
    loads = [pltpu.make_async_copy(src, dst, table_sem.at[i]) for i, (src, dst) in enumerate(moves)]
    for load in loads[:4]:
        load.start()

    barrier = pltpu.get_barrier_semaphore()
    z = lax.rem(r, 2) * 4 + lax.rem(lax.div(b, 2), 4)
    x = lax.div(b, 8)

    def place(px, py, pz, pc):
        return (py * 2 + lax.div(pz, 4)) * BULKS + px * 8 + lax.rem(pz, 4) * 2 + pc

    plane_peers = [place(lax.rem(x + i, 4), lax.rem(y + j, 4), z, core) for i in range(4) for j in range(4) if i + j]
    line_peers = [place(x, y, lax.rem(z + i, 8), lax.rem(core + j, 2)) for i in range(8) for j in range(2) if i + j]
    for peer in plane_peers + line_peers:
        pl.semaphore_signal(barrier, inc=1, device_id=at(peer), device_id_type=MESH)
    for load in loads[4:]:
        load.start()

    loads[0].wait()
    loads[1].wait()
    lane = lax.broadcasted_iota(jnp.int32, (DEVICES, 128), 1)
    for q in range(2):
        rows = jnp.concatenate([charge[:, 4 * q + j, :] for j in range(4)], axis=0)
        c_hi, c_lo = parts(rows)
        spec = dot3(fwd[0], fwd[1], c_hi, c_lo, ((1,), (1,)))
        if q == 1:
            pl.semaphore_wait(barrier, len(plane_peers) + len(line_peers))
            for peer in line_peers:
                pl.semaphore_signal(gate, inc=1, device_id=at(peer), device_id_type=MESH)
        for p in range(2):
            re = spec[:DEVICES, 128 * p : 128 * (p + 1)]
            im = spec[DEVICES:, 128 * p : 128 * (p + 1)]
            k = 4 * q + 2 * p
            sbuf[pl.ds(k, DEVICES, stride=8), :] = jnp.where(lane < 64, re, pltpu.roll(im, 64, 1))
            sbuf[pl.ds(k + 1, DEVICES, stride=8), :] = jnp.where(lane < 64, pltpu.roll(re, 64, 1), im)

    loads[2].wait()
    loads[3].wait()
    lab[:, :N] = shells[pl.ds(jnp.where(b < BULKS // 2, r, 8 - r), 1), :]
    lab_src[...] = shells[0:1, :]

    pltpu.make_async_copy(tile(sbuf, m), tile(rbuf, m), rsem.at[y]).start()

    def send(d):
        push(tile(sbuf, d), tile(rbuf, m), d, ssem, rsem.at[y]).start()

    for peer in line_peers + plane_peers:
        send(peer)
    pl.semaphore_wait(gate, len(line_peers))
    for c in range(2):
        def across(k, carry, c=c):
            base = lax.rem(y + lax.div(k, 4), 4) * 2 * BULKS + lax.rem(x + lax.rem(k, 4), 4) * 8 + c

            def along(j, inner):
                pz = lax.rem(z + j, 8)
                send(base + lax.div(pz, 4) * BULKS + lax.rem(pz, 4) * 2)
                return inner

            return lax.fori_loop(jnp.where(core == c, 1, 0), 8, along, carry)

        lax.fori_loop(1, 16, across, 0)

    @pl.when(feeder)
    def _():
        push(lab_src, lab_far, 0, lssem, lrsem).start()

    loads[4].wait()
    for s in range(8):
        hi, lo = parts(g32[s])
        g_hi[s] = hi
        g_lo[s] = lo
    loads[5].wait()
    loads[6].wait()

    @pl.when(feeder)
    def _():
        drain(lab_src, lssem)

    @pl.when(first)
    def _():
        drain(lab_far, lrsem)
        lab[:, N:] = lab_far[...]

    @pl.when(jnp.logical_not(first))
    def _():
        lab[:, N:] = lab[:, :N]

    spec_ref[...] = jnp.zeros_like(spec_ref)

    def gather(t, carry):
        g = lax.rem(y + 4 - t, 4)
        drain(rbuf.at[pl.ds(pl.multiple_of(g * 512, 512), 512), :], rsem.at[g])
        rows = [rbuf[pl.ds(pl.multiple_of(g * 512 + h * NZ, NZ), NZ), :] for h in range(2)]
        hi, lo = parts(jnp.concatenate(rows, axis=1))
        deep = pl.ds(pl.multiple_of(g * 256, 256), 256)
        spec_ref[...] += dot3(hi, lo, mat[0, deep, :], mat[1, deep, :])
        return carry

    lax.fori_loop(0, 4, gather, 0, unroll=True)

    def solve(t, carry):
        cols = pl.ds(pl.multiple_of(t * 256, 256), 256)
        s_hi, s_lo = parts(spec_ref[:, cols])
        label = lab[:, cols]
        acc = jnp.zeros((NZ, 256), jnp.float32)
        for s in range(8):
            mask = label == s
            m_hi = jnp.where(mask, s_hi, jnp.zeros_like(s_hi))
            m_lo = jnp.where(mask, s_lo, jnp.zeros_like(s_lo))
            acc = acc + dot3(g_hi[s], g_lo[s], m_hi, m_lo)
        hi, lo = parts(acc)
        v_hi[:, cols] = hi
        v_lo[:, cols] = lo
        return carry

    lax.fori_loop(0, 4, solve, 0, unroll=True)

    spot = core * HALF + pair
    for g in range(2):
        cols = slice(g * 512, (g + 1) * 512)
        back = dot3(v_hi[...], v_lo[...], mat_t[0, :, cols], mat_t[1, :, cols])
        for h in range(4):
            obuf[(4 * g + h) * NZ : (4 * g + h + 1) * NZ, :] = back[:, h * 128 : (h + 1) * 128]

    pltpu.make_async_copy(tile(obuf, m), tile(home, spot), hrsem.at[core]).start()

    def give(i, carry):
        d = lax.rem(m + i, DEVICES)
        push(tile(obuf, d), tile(home, spot), d, hssem, hrsem.at[core]).start()
        return carry

    lax.fori_loop(1, 32, give, 0)
    for g in range(ROWS):
        for p in range(4):
            ebuf[4 * g + p] = obuf[pl.ds(g * NZ + planes[p], 1), :]

    def plate(k, carry):
        d = lax.div(k, 4) * BULKS + HOT * lax.rem(k, 4)

        @pl.when(d != m)
        def _():
            push(ebuf.at[k], erecv.at[m], d, essem, ersem).start()

        @pl.when(d == m)
        def _():
            pltpu.make_async_copy(ebuf.at[k], erecv.at[m], ersem).start()

        return carry

    lax.fori_loop(0, 32, plate, 0, unroll=4)
    lax.fori_loop(32, DEVICES, give, 0, unroll=4)
    loads[7].wait()
    loads[8].wait()

    def regain(c):
        drain(home.at[pl.ds(c * 8 * HALF, 8 * HALF), :], hrsem.at[c])
        re, im = [], []
        for k in range(8):
            flip = jnp.transpose(home[pl.ds(c * 8 * HALF + k, HALF, stride=8), :])
            re.append(flip[:64])
            im.append(flip[64:])
        w_hi, w_lo = parts(jnp.concatenate([jnp.concatenate(re, axis=0), jnp.concatenate(im, axis=0)], axis=1))
        return dot3(w_hi, w_lo, inv_v[0, c], inv_v[1, c])

    field_ref[...] = regain(0)

    @pl.when(hot)
    def _():
        drain(erecv, ersem)
        e_hi, e_lo = parts(erecv[...].reshape(DEVICES, 128))
        both = dot3(inv_t_v[0], inv_t_v[1], e_hi, e_lo)
        near = (both[:N] + pltpu.roll(both[N:], 64, 1)).reshape(BULKS, 16, 128)
        far = (pltpu.roll(both[:N], 64, 1) + both[N:]).reshape(BULKS, 16, 128)
        side = lax.broadcasted_iota(jnp.int32, (BULKS, 8, 128), 2)
        eout[...] = jnp.where(side < 64, near[:, :8], far[:, 8:]).reshape(8 * BULKS, 128)
        p = lax.div(b, HOT)

        def spread(j, c):
            d = r * BULKS + lax.rem(b + j, BULKS)
            push(tile(eout, lax.rem(d, BULKS)), elrecv.at[p], d, elssem, elrsem).start()
            return c

        pltpu.make_async_copy(tile(eout, b), elrecv.at[p], elrsem).start()
        lax.fori_loop(1, BULKS, spread, 0)

    rest = regain(1)
    for k in range(8):
        out[:, k, :] = field_ref[64 * k : 64 * (k + 1), :] + rest[64 * k : 64 * (k + 1)]

    drain(elrecv, elrsem)
    electrodes[:, :8, :] = elrecv[:, :, :64]
    electrodes[:, 8:, :] = elrecv[:, :, 64:]

    drain(sbuf.at[pl.ds(0, 8 * (DEVICES - 1)), :], ssem)
    drain(obuf.at[pl.ds(0, 8 * (DEVICES - 1)), :], hssem)
    drain(ebuf.at[pl.ds(0, 31)], essem)

    @pl.when(jnp.logical_not(hot))
    def _():
        drain(ebuf.at[0], essem)

    @pl.when(hot)
    def _():
        drain(eout.at[pl.ds(0, 8 * (BULKS - 1)), :], elssem)


def local(charge, green, shells, planes):
    fwd, mats, mats_t, inv, inv_t = (jnp.asarray(t) for t in tables())
    f32, bf16, i32 = jnp.float32, jnp.bfloat16, jnp.int32
    vmem, hbm = pl.BlockSpec(memory_space=pltpu.VMEM), pl.BlockSpec(memory_space=pltpu.HBM)
    dma = pltpu.SemaphoreType.DMA
    operands = (charge, fwd, shells, planes, green, mats, mats_t, inv, inv_t)
    field, plates = pl.pallas_call(
        kernel,
        out_shape=(
            jax.ShapeDtypeStruct(charge.shape, f32),
            jax.ShapeDtypeStruct((4, N // BULKS, N // ROWS), f32),
        ),
        in_specs=[hbm] * 9,
        out_specs=(vmem, vmem),
        scratch_shapes=[
            pltpu.VMEM(charge.shape, f32),
            pltpu.VMEM(fwd.shape, bf16),
            pltpu.VMEM(shells.shape, i32),
            pltpu.SMEM(planes.shape, i32),
            pltpu.VMEM((8 * DEVICES, 128), f32),
            pltpu.VMEM((8 * DEVICES, 128), f32),
            pltpu.VMEM((8 * DEVICES, 128), f32),
            pltpu.VMEM((8 * DEVICES, 128), f32),
            pltpu.VMEM(mats.shape[1:], bf16),
            pltpu.VMEM(mats.shape[1:], bf16),
            pltpu.VMEM(inv.shape, bf16),
            pltpu.VMEM(inv_t.shape, bf16),
            pltpu.VMEM((8, NZ, NZ), f32),
            pltpu.VMEM((8, NZ, NZ), bf16),
            pltpu.VMEM((8, NZ, NZ), bf16),
            pltpu.VMEM((NZ, 2 * N), f32),
            pltpu.VMEM((NZ, 2 * N), bf16),
            pltpu.VMEM((NZ, 2 * N), bf16),
            pltpu.VMEM((N, N), f32),
            pltpu.VMEM((1, 2 * N), i32),
            pltpu.VMEM((1, N), i32),
            pltpu.VMEM((1, N), i32),
            pltpu.VMEM((32, 1, 128), f32),
            pltpu.VMEM((DEVICES, 1, 128), f32),
            pltpu.VMEM((8 * BULKS, 128), f32),
            pltpu.VMEM((4, 8, 128), f32),
            pltpu.SemaphoreType.REGULAR,
            dma((9,)),
            dma,
            dma((4,)),
            dma,
            dma((2,)),
        ]
        + [dma] * 6,
        compiler_params=pltpu.CompilerParams(
            collective_id=0, has_side_effects=True, vmem_limit_bytes=48 * 1024 * 1024
        ),
    )(*(pltpu.with_memory_space_constraint(a, pltpu.HBM) for a in operands))
    return field, jnp.transpose(plates, (0, 2, 1))


def solution(mesh):
    placed = (P("row", "bulk", None), P(), P("bulk", None), P())
    return jax.shard_map(
        local,
        mesh=mesh,
        in_specs=placed,
        out_specs=(P("row", "bulk", None), P(None, "row", "bulk")),
        check_vma=False,
    )
```
